32 devices in a mesh: batch: 4 (over z), seq: 8 (over y, x, core).
Axes of the slice: x: 2, y: 2, z: 4, core: 2. Of those that a mesh axis runs over, the one named last changes fastest.
Arguments:
- tokens: bfloat16 [4, 1024, 2048], P('batch', 'seq'), may hold values from -6 to 6
- positions: int32 [4, 1024], P('batch', 'seq'), may hold values from 0 to 1535, as said below
- gain_attn: float32 [2048], P(('batch', 'seq')), may hold values from 0.1 to 1.9
- query_weight: float32 [2048, 2048], P(('batch', 'seq')), may hold values from -0.1875 to 0.1875
- key_weight: float32 [2048, 2048], P(('batch', 'seq')), may hold values from -0.1875 to 0.1875
- value_weight: float32 [2048, 2048], P(('batch', 'seq')), may hold values from -0.125 to 0.125
- out_weight: float32 [2048, 2048], P(None, ('batch', 'seq')), may hold values from -0.1875 to 0.1875
- gain_ffn: float32 [2048], P(('batch', 'seq')), may hold values from 0.1 to 1.9
- gate_weight: float32 [2048, 8192], P(('batch', 'seq')), may hold values from -0.125 to 0.125
- up_weight: float32 [2048, 8192], P(('batch', 'seq')), may hold values from -0.125 to 0.125
- down_weight: float32 [8192, 2048], P(None, ('batch', 'seq')), may hold values from -0.0625 to 0.0625
- cotangent: bfloat16 [4, 1024, 2048], P('batch', 'seq'), may hold values from -6 to 6
Outputs:
- layer_out: bfloat16 [4, 1024, 2048], P('batch', 'seq')
- input_grad: bfloat16 [4, 1024, 2048], P('batch', 'seq')
- attn_mass: float32 [4, 1024], P('batch', 'seq')
- gain_attn_grad: float32 [2048], P(('batch', 'seq'))
- query_grad: float32 [2048, 2048], P(('batch', 'seq'))
- key_grad: float32 [2048, 2048], P(('batch', 'seq'))
- value_grad: float32 [2048, 2048], P(('batch', 'seq'))
- out_grad: float32 [2048, 2048], P(None, ('batch', 'seq'))
- gain_ffn_grad: float32 [2048], P(('batch', 'seq'))
- gate_grad: float32 [2048, 8192], P(('batch', 'seq'))
- up_grad: float32 [2048, 8192], P(('batch', 'seq'))
- down_grad: float32 [8192, 2048], P(None, ('batch', 'seq'))
The draws below stay inside these ranges and needn't reach their ends.
Inputs may be any that keep to these rules, and one draw needn't show every extreme that they name: Along each sequence the positions start at 0 and grow by 1 or 2 from token to token, by 2 at exactly 512 steps.
All inputs are finite; a program needn't handle non-finite values.
Results may differ from the reference program's by a relative error of at most 0.018.
The reference program's roundings to bfloat16 on the way count: a program that leaves them out, or rounds other values in their place, can miss the bound.
Values may be sent and summed in bfloat16 or wider, within the bound.
No kernel may reach another device: no remote copies, remote signals or barrier semaphores. Data moves between devices by JAX's collectives and lax.ppermute only.
A program may use at most 768 MiB of HBM per device.

```python
import math
import jax
import jax.numpy as jnp
from jax import lax

D = 2048
HEADS = 16
HD = 128
FF = 8192
NB = 4
LEN = 1024


def draw_positions(key, part):
    key = jax.random.fold_in(key, 11)
    row_keys = jax.random.split(key, NB)

    def one_row(row_key):
        order = jax.random.permutation(row_key, LEN - 1)
        jumps = (order < LEN // 2).astype(jnp.int32)
        jumps = jnp.concatenate([jumps, jnp.zeros((1,), jnp.int32)])
        return jnp.arange(LEN, dtype=jnp.int32) + jnp.cumsum(jumps) - jumps
    return jax.vmap(one_row)(row_keys)


def level_of(stream_key, dims, cuts, smallest, largest):
    loudness = 1.0
    for axis_at, blocks in cuts:
        steps = jax.random.uniform(jax.random.fold_in(jax.random.fold_in(stream_key, 6), axis_at), (blocks,), jnp.float32, smallest / len(cuts), largest / len(cuts))
        loudness = loudness * jnp.repeat(jnp.exp(steps), dims[axis_at] // blocks).reshape((-1,) + (1,) * (len(dims) - 1 - axis_at))
    return loudness


def centred(stream_key, shape, deviation, limit, shards=(), kind=jnp.bfloat16):
    drawn = jax.random.normal(stream_key, shape, jnp.float32) * deviation
    if len(shards) > 0:
        drawn = level_of(stream_key, shape, shards, -0.22, 0.18) * drawn
    return jnp.clip(drawn, min=-limit, max=limit).astype(kind)


def setup_inputs(seed: int = 0) -> dict:
    splits = jax.random.split(jax.random.key(seed), 13)
    return {
        "tokens": centred(splits[0], (NB, LEN, D), 1.0, 6.0, ((0, 4), (1, 8))),
        "positions": draw_positions(jax.random.fold_in(splits[12], 71), 0),
        "gain_attn": jnp.clip(1.0 + 0.18 * jax.random.normal(splits[2], (D,), jnp.float32), 0.1, 1.9),
        "query_weight": centred(splits[3], (D, D), (D // 2) ** -0.5, 0.1875, ((0, 32),), jnp.float32),
        "key_weight": centred(splits[4], (D, D), (D // 2) ** -0.5, 0.1875, ((0, 32),), jnp.float32),
        "value_weight": centred(splits[5], (D, D), D ** -0.5, 0.125, ((0, 32),), jnp.float32),
        "out_weight": centred(splits[6], (D, D), (D // 2) ** -0.5, 0.1875, ((1, 32),), jnp.float32),
        "gain_ffn": jnp.clip(1.0 + 0.18 * jax.random.normal(splits[7], (D,), jnp.float32), 0.1, 1.9),
        "gate_weight": centred(splits[8], (D, FF), D ** -0.5, 0.125, ((0, 32),), jnp.float32),
        "up_weight": centred(splits[9], (D, FF), D ** -0.5, 0.125, ((0, 32),), jnp.float32),
        "down_weight": centred(splits[10], (FF, D), FF ** -0.5, 0.0625, ((1, 32),), jnp.float32),
        "cotangent": centred(splits[11], (NB, LEN, D), 1.0, 6.0, ((0, 4), (1, 8))),
    }


epsilon = 1e-05
rope_base = 10000.0
score_bias = -math.log(4096.0)

@jax.custom_vjp
def low(v):
    return lax.optimization_barrier(v.astype(jnp.bfloat16)).astype(jnp.float32)

@jax.custom_vjp
def low_back(v):
    return v

def low_keep(v):
    return (low(v), None)

def low_pass(kept, grad):
    return (grad,)

def back_keep(v):
    return (v, None)

def back_low(kept, grad):
    return (low(grad),)
low.defvjp(low_keep, low_pass)
low_back.defvjp(back_keep, back_low)

def product(left, right):
    return jnp.dot(left, right, precision=lax.Precision.HIGHEST)

def norm_scale(values):
    return lax.rsqrt(lax.optimization_barrier(jnp.mean(values * values, axis=-1, keepdims=True)) + epsilon)

def rotate(values, seq_pos):
    length = values.shape[0]
    shaped = values.reshape(length, HEADS, HD)
    half_size = HD // 2
    frequency = jnp.exp(jnp.arange(half_size).astype(values.dtype) * (-2.0 * math.log(rope_base) / HD))
    angles = seq_pos.astype(values.dtype)[:, None] * frequency[None, :]
    cosine = jnp.cos(angles)[:, None, :]
    sine_part = jnp.sin(angles)[:, None, :]
    first_part = shaped[..., :half_size]
    second_part = shaped[..., half_size:]
    return jnp.concatenate([first_part * cosine - second_part * sine_part, second_part * cosine + first_part * sine_part], axis=-1)

def attend(queries, key_rows, values, seq_pos):
    length = queries.shape[0]
    block_size = min(512, length)
    block_count = length // block_size
    query_blocks = queries.reshape(block_count, block_size, HEADS, HD)
    pos_blocks = seq_pos.reshape(block_count, block_size)
    score_scale = 1.0 / math.sqrt(HD)

    def one_block(step_items):
        query_block, query_pos = step_items
        scores = jnp.einsum('qhd,khd->hqk', query_block, key_rows, precision=lax.Precision.HIGHEST) * score_scale + score_bias
        scores = low_back(scores)
        visible = seq_pos[None, None, :] <= query_pos[None, :, None]
        weights = jnp.where(visible, jax.nn.sigmoid(scores), 0.0)
        output = jnp.einsum('hqk,khd->qhd', low(weights), values, precision=lax.Precision.HIGHEST)
        attn_mass = lax.optimization_barrier(jnp.sum(weights, axis=(0, 2))) / HEADS
        return (output, attn_mass)
    outputs, masses = lax.map(jax.checkpoint(one_block), (query_blocks, pos_blocks))
    return (outputs.reshape(length, HEADS * HD), masses.reshape(length))

def block_forward(inputs, seq_pos, gain_attn, query_weight, key_weight, value_weight, out_weight, gain_ffn, gate_weight, up_weight, down_weight):
    length = inputs.shape[0]
    normed = low(inputs * norm_scale(inputs) * low(gain_attn))
    query_raw = low_back(product(normed, low(query_weight)))
    key_raw = low_back(product(normed, low(key_weight)))
    values = low(low_back(product(normed, low(value_weight))))
    queries = low(rotate(query_raw, seq_pos))
    key_rows = low(rotate(key_raw, seq_pos))
    attended, attn_mass = attend(queries, key_rows, values.reshape(length, HEADS, HD), seq_pos)
    attended = low(low_back(attended))
    hidden_state = inputs + low_back(product(attended, low(out_weight)))
    normed_ffn = low(hidden_state * norm_scale(hidden_state) * low(gain_ffn))
    gate_proj = low_back(product(normed_ffn, low(gate_weight)))
    up_proj = low_back(product(normed_ffn, low(up_weight)))
    activation = low(jax.nn.silu(gate_proj) * up_proj)
    return (hidden_state + low_back(product(activation, low(down_weight))), attn_mass)

def reference(tokens, positions, gain_attn, query_weight, key_weight, value_weight, out_weight, gain_ffn, gate_weight, up_weight, down_weight, cotangent):
    parameters = (gain_attn, query_weight, key_weight, value_weight, out_weight, gain_ffn, gate_weight, up_weight, down_weight)

    def one_sequence(totals, step_items):
        inputs, seq_pos, seq_cot = step_items

        def forward(inputs_f, *weight_list):
            return block_forward(inputs_f, seq_pos, *weight_list)
        outputs, pullback, attn_mass = jax.vjp(forward, inputs.astype(jnp.float32), *parameters, has_aux=True)
        gradients = pullback(seq_cot.astype(jnp.float32))
        totals = jax.tree.map(lambda left, right: left + right, totals, tuple(gradients[1:]))
        return (totals, (outputs.astype(jnp.bfloat16), gradients[0].astype(jnp.bfloat16), attn_mass))
    zeros_start = tuple((jnp.zeros_like(item) for item in parameters))
    totals, (layer_out, input_grad, attn_mass) = lax.scan(one_sequence, zeros_start, (tokens, positions, cotangent))
    return (layer_out, input_grad, attn_mass, totals[0], totals[1], totals[2], totals[3], totals[4], totals[5], totals[6], totals[7], totals[8])
```

```python
import math

import jax
import jax.numpy as jnp
from jax import lax
from jax.sharding import PartitionSpec as P

HD = 128
epsilon = 1e-05
rope_base = 10000.0
score_bias = -math.log(4096.0)
score_scale = 1.0 / math.sqrt(HD)
f32 = jnp.float32
bf16 = jnp.bfloat16
PAD = 16
CHUNKS = 4


def dot(left, right):
    return jnp.dot(left, right, preferred_element_type=f32)


def dot_t(left, right):
    return lax.dot_general(left, right, (((1,), (1,)), ((), ())), preferred_element_type=f32)


def t_dot(left, right):
    return lax.dot_general(left, right, (((0,), (0,)), ((), ())), preferred_element_type=f32)


def norm_scale(values):
    return lax.rsqrt(jnp.mean(values * values, axis=-1, keepdims=True) + epsilon)


def norm_back(grad_normed, unit_rows, scale_rows, gain_vec):
    grad_unit = grad_normed * gain_vec
    return scale_rows * (
        grad_unit - unit_rows * jnp.mean(grad_unit * unit_rows, axis=-1, keepdims=True)
    )


def angles_of(seq_pos):
    half_size = HD // 2
    frequency = jnp.exp(
        jnp.arange(half_size).astype(f32) * (-2.0 * math.log(rope_base) / HD)
    )
    angles = seq_pos.astype(f32)[:, None] * frequency[None, :]
    return jnp.cos(angles)[None], jnp.sin(angles)[None]


def rotate(heads, cosine, sine):
    half_size = HD // 2
    first = heads[..., :half_size]
    second = heads[..., half_size:]
    return jnp.concatenate(
        [first * cosine - second * sine, second * cosine + first * sine], axis=-1
    )


def to_heads(rows):
    return rows.reshape(rows.shape[0], -1, HD).transpose(1, 0, 2)


def from_heads(heads):
    return heads.transpose(1, 0, 2).reshape(heads.shape[1], -1)


def body(
    tokens,
    positions,
    gain_attn,
    query_weight,
    key_weight,
    value_weight,
    out_weight,
    gain_ffn,
    gate_weight,
    up_weight,
    down_weight,
    cotangent,
):
    ns = lax.axis_size("seq")
    nb = lax.axis_size("batch")
    rows = query_weight.shape[0]
    width = query_weight.shape[1]
    hidden = gate_weight.shape[1]
    head_cols = width // ns
    ffn_cols = hidden // (ns * CHUNKS)

    def slices(weight, parts=1):
        cut = weight.astype(bf16).reshape(rows, ns, parts, -1)
        return cut.transpose(2, 1, 0, 3)

    def swap(blocks):
        return lax.all_to_all(blocks, "seq", split_axis=0, concat_axis=0, tiled=True)

    def gather_z(block):
        return lax.all_gather(block, "batch", axis=0, tiled=True)

    def gather_s(block):
        return lax.all_gather(block, "seq", axis=0, tiled=True)

    def scatter_z(full):
        return lax.psum_scatter(full, "batch", scatter_dimension=0, tiled=True)

    def scatter_s(full):
        return lax.psum_scatter(full, "seq", scatter_dimension=0, tiled=True)

    qkv_blocks = jnp.concatenate(
        [slices(query_weight)[0], slices(key_weight)[0], slices(value_weight)[0]], axis=2
    )
    gains = jnp.stack([gain_attn.astype(bf16), gain_ffn.astype(bf16)])
    gain_rows = jnp.pad(gains, ((0, PAD - 2), (0, 3 * head_cols - rows)))
    gain_rows = jnp.broadcast_to(gain_rows[None], (ns,) + gain_rows.shape)
    qkv_blocks = swap(jnp.concatenate([qkv_blocks, gain_rows], axis=1))
    full_blocks = gather_z(qkv_blocks)
    w_qkv = full_blocks[:, :rows].reshape(nb * ns * rows, 3 * head_cols)
    gain_one = full_blocks[:, rows, :rows].reshape(-1).astype(f32)
    gain_two = full_blocks[:, rows + 1, :rows].reshape(-1).astype(f32)

    out_blocks = swap(slices(out_weight.T)[0])
    w_out = gather_z(out_blocks.reshape(ns * rows, head_cols))

    ffn_blocks = jnp.concatenate(
        [slices(gate_weight, CHUNKS), slices(up_weight, CHUNKS), slices(down_weight.T, CHUNKS)],
        axis=3,
    )
    w_ffn = [
        gather_z(swap(ffn_blocks[c]).reshape(ns * rows, 3 * ffn_cols)) for c in range(CHUNKS)
    ]

    x_own = tokens[0]
    x_own_f = x_own.astype(f32)
    x_all = gather_s(x_own)
    seq_pos = gather_s(positions[0])
    dy_all = gather_s(cotangent[0])
    length = x_all.shape[0]
    unit_one = x_all.astype(f32)
    unit_one = unit_one * norm_scale(unit_one)
    normed = (unit_one * gain_one).astype(bf16)
    cosine, sine = angles_of(seq_pos)
    qkv = dot(normed, w_qkv)
    queries = rotate(to_heads(qkv[:, :head_cols]), cosine, sine).astype(bf16)
    keys = rotate(to_heads(qkv[:, head_cols : 2 * head_cols]), cosine, sine).astype(bf16)
    values = to_heads(qkv[:, 2 * head_cols :]).astype(bf16)
    index = jnp.arange(length, dtype=jnp.int32)
    visible = (index[None, :] <= index[:, None])[None]
    scores = (
        jnp.einsum("hqd,hkd->hqk", queries, keys, preferred_element_type=f32) * score_scale
        + score_bias
    )
    weights = jnp.where(visible, jax.nn.sigmoid(scores), 0.0)
    weights_low = weights.astype(bf16)
    attended = from_heads(
        jnp.einsum("hqk,hkd->hqd", weights_low, values, preferred_element_type=f32).astype(bf16)
    )
    heads_total = width // HD
    attn_mass = scatter_s(jnp.sum(weights, axis=(0, 2)) * (1.0 / heads_total))

    hidden_own = x_own_f + scatter_s(dot_t(attended, w_out).astype(bf16)).astype(f32)
    scale_two = norm_scale(hidden_own)
    unit_two = hidden_own * scale_two
    normed_ffn = gather_s((unit_two * gain_two).astype(bf16))

    out_part = 0.0
    back_part = 0.0
    ffn_sums = []
    for c in range(CHUNKS):
        w_gate = w_ffn[c][:, :ffn_cols]
        w_up = w_ffn[c][:, ffn_cols : 2 * ffn_cols]
        w_down = w_ffn[c][:, 2 * ffn_cols :]
        gate = dot(normed_ffn, w_gate)
        up = dot(normed_ffn, w_up)
        grad_act = dot(dy_all, w_down)
        sig = jax.nn.sigmoid(gate)
        silu = gate * sig
        act = (silu * up).astype(bf16)
        grad_gate = (grad_act * up * sig * (1.0 + gate * (1.0 - sig))).astype(bf16)
        grad_up = (grad_act * silu).astype(bf16)
        out_part = out_part + dot_t(act, w_down)
        back_part = back_part + dot_t(
            jnp.concatenate([grad_gate, grad_up], axis=1), w_ffn[c][:, : 2 * ffn_cols]
        )
        sums = jnp.concatenate(
            [
                t_dot(normed_ffn, grad_gate).astype(bf16),
                t_dot(normed_ffn, grad_up).astype(bf16),
                t_dot(dy_all, act).astype(bf16),
            ],
            axis=1,
        )
        ffn_sums.append(scatter_z(sums))
    grad_normed_two = scatter_s(back_part.astype(bf16)).astype(f32)
    layer_out = (hidden_own + scatter_s(out_part.astype(bf16)).astype(f32)).astype(bf16)
    grad_hidden = cotangent[0].astype(f32) + norm_back(
        grad_normed_two, unit_two, scale_two, gain_two
    )
    gain_two_part = jnp.sum(grad_normed_two * unit_two, axis=0)

    branch = gather_s(grad_hidden.astype(bf16))
    grad_heads = to_heads(dot(branch, w_out).astype(bf16))
    out_sum = t_dot(branch, attended).astype(bf16)
    grad_weights = jnp.einsum("hqd,hkd->hqk", grad_heads, values, preferred_element_type=f32)
    grad_scores = (grad_weights * weights * (1.0 - weights)).astype(bf16)
    grad_values = jnp.einsum("hqk,hqd->hkd", weights_low, grad_heads, preferred_element_type=f32)
    grad_keys = (
        jnp.einsum("hqk,hqd->hkd", grad_scores, queries, preferred_element_type=f32) * score_scale
    )
    grad_queries = (
        jnp.einsum("hqk,hkd->hqd", grad_scores, keys, preferred_element_type=f32) * score_scale
    )
    grad_qkv = jnp.concatenate(
        [
            from_heads(rotate(grad_queries, cosine, -sine).astype(bf16)),
            from_heads(rotate(grad_keys, cosine, -sine).astype(bf16)),
            from_heads(grad_values.astype(bf16)),
        ],
        axis=1,
    )
    qkv_sum = t_dot(normed, grad_qkv).astype(bf16)
    normed_part = dot_t(grad_qkv, w_qkv)
    gain_one_part = jnp.sum(normed_part * unit_one, axis=0)
    grad_normed = scatter_s(normed_part.astype(bf16)).astype(f32)
    scale_one = norm_scale(x_own_f)
    input_grad = (
        grad_hidden + norm_back(grad_normed, x_own_f * scale_one, scale_one, gain_one)
    ).astype(bf16)

    attn_cols = 3 * head_cols
    gain_parts = jnp.stack([gain_one_part, gain_two_part]).astype(bf16)
    gain_parts = gain_parts.reshape(2, nb, ns, rows).transpose(1, 2, 0, 3)
    gain_parts = jnp.pad(gain_parts, ((0, 0), (0, 0), (0, PAD - 2), (0, attn_cols - rows)))
    attn_sums = jnp.concatenate(
        [qkv_sum.reshape(nb, ns, rows, attn_cols), gain_parts], axis=2
    ).reshape(nb * ns * (rows + PAD), attn_cols)
    attn_sums = swap(scatter_z(attn_sums).reshape(ns, rows + PAD, attn_cols))
    gain_grads = jnp.sum(attn_sums[:, rows : rows + 2, :rows].astype(f32), axis=0)

    def unslice(blocks):
        return blocks.astype(f32).transpose(1, 0, 2).reshape(rows, -1)

    attn_grads = [
        unslice(attn_sums[:, :rows, i * head_cols : (i + 1) * head_cols]) for i in range(3)
    ]
    out_grad = unslice(swap(scatter_z(out_sum).reshape(ns, rows, head_cols))).T
    ffn_back = jnp.stack(
        [swap(part.reshape(ns, rows, 3 * ffn_cols)) for part in ffn_sums], axis=1
    )
    ffn_grads = [
        ffn_back[..., i * ffn_cols : (i + 1) * ffn_cols]
        .astype(f32)
        .transpose(2, 0, 1, 3)
        .reshape(rows, hidden)
        for i in range(3)
    ]
    return (
        layer_out[None],
        input_grad[None],
        attn_mass[None],
        gain_grads[0],
        attn_grads[0],
        attn_grads[1],
        attn_grads[2],
        out_grad,
        gain_grads[1],
        ffn_grads[0],
        ffn_grads[1],
        ffn_grads[2].T,
    )


def solution(mesh):
    both = ("batch", "seq")
    token_spec = P("batch", "seq", None)
    row_spec = P(both, None)
    col_spec = P(None, both)
    return jax.shard_map(
        body,
        mesh=mesh,
        in_specs=(
            token_spec,
            P("batch", "seq"),
            P(both),
            row_spec,
            row_spec,
            row_spec,
            col_spec,
            P(both),
            row_spec,
            row_spec,
            col_spec,
            token_spec,
        ),
        out_specs=(
            token_spec,
            token_spec,
            P("batch", "seq"),
            P(both),
            row_spec,
            row_spec,
            row_spec,
            col_spec,
            P(both),
            row_spec,
            row_spec,
            col_spec,
        ),
        check_vma=False,
    )
```

```python
import functools
import math

import jax
import jax.numpy as jnp
from jax import lax
from jax.experimental import pallas as pl
from jax.experimental.pallas import tpu as pltpu
from jax.sharding import PartitionSpec as P

HD = 128
LANES = 128
epsilon = 1e-05
rope_base = 10000.0
score_bias = -math.log(4096.0)
score_scale = 1.0 / math.sqrt(HD)
f32 = jnp.float32
bf16 = jnp.bfloat16
CHUNKS = 2
TILE = 256
MIB = 1 << 20


def dot(left, right):
    return jnp.dot(left, right, preferred_element_type=f32)


def dot_t(left, right):
    return lax.dot_general(left, right, (((1,), (1,)), ((), ())), preferred_element_type=f32)


def t_dot(left, right):
    return lax.dot_general(left, right, (((0,), (0,)), ((), ())), preferred_element_type=f32)


def norm_scale(values):
    return lax.rsqrt(jnp.mean(values * values, axis=-1, keepdims=True) + epsilon)


def norm_back(grad_normed, unit_rows, scale_rows, gain_vec):
    grad_unit = grad_normed * gain_vec
    return scale_rows * (
        grad_unit - unit_rows * jnp.mean(grad_unit * unit_rows, axis=-1, keepdims=True)
    )


def columns(array, at, cols):
    return pl.BlockSpec((array.shape[0], cols), lambda *_: (0, at), pipeline_mode=pl.Buffered(1))


def whole(shape):
    zeros = (0,) * len(shape)
    return pl.BlockSpec(shape, lambda *_: zeros, pipeline_mode=pl.Buffered(1))


def rows_of(tile, cols):
    return pl.BlockSpec((tile, cols), lambda i, *_: (i, 0))


def call(kernel, steps, ins, in_specs, outs, out_specs, flops, vmem=60, scalars=0):
    size = sum(math.prod(a.shape) * a.dtype.itemsize for a in (*ins, *outs))
    result = pl.pallas_call(
        kernel,
        grid_spec=pltpu.PrefetchScalarGridSpec(
            num_scalar_prefetch=scalars,
            grid=(steps,),
            in_specs=in_specs,
            out_specs=out_specs,
        ),
        out_shape=outs,
        compiler_params=pltpu.CompilerParams(
            dimension_semantics=("arbitrary",), vmem_limit_bytes=vmem * MIB
        ),
        cost_estimate=pl.CostEstimate(flops=flops, bytes_accessed=size, transcendentals=0),
    )(*ins)
    return result[0] if len(outs) == 1 else result


def pack_kernel(plans, *refs):
    ins, outs = refs[: -len(plans)], refs[-len(plans) :]
    for plan, out_ref in zip(plans, outs):
        at = 0
        for m, part, parts in plan:
            cols = ins[m].shape[1] // parts
            value = ins[m][:, part * cols : (part + 1) * cols]
            out_ref[0, :, at : at + cols] = value.astype(bf16)
            at += cols


def pack(arrays, plans, ns, marks=None):
    rows = arrays[0].shape[0]
    specs = [pl.BlockSpec((rows, a.shape[1] // ns), lambda i: (0, i)) for a in arrays]
    widths = [a.shape[1] // ns for a in arrays]
    if marks is not None:
        plans = [plan + [(len(arrays), 0, 1)] for plan in plans]
        arrays = arrays + (marks,)
        specs.append(whole(marks.shape))
        widths.append(marks.shape[1])
    cols = [sum(widths[m] // parts for m, _, parts in plan) for plan in plans]
    return call(
        functools.partial(pack_kernel, plans),
        ns,
        arrays,
        specs,
        [jax.ShapeDtypeStruct((ns, rows, n), bf16) for n in cols],
        [pl.BlockSpec((1, rows, n), lambda i: (i, 0, 0)) for n in cols],
        0,
    )


def turn(values, cosine, sine):
    return values * cosine + pltpu.roll(values, HD // 2, 1) * sine


def attend_kernel(
    heads_all, q_ref, k_ref, v_ref, cos_ref, sin_ref, col_ref, row_ref, qo, ko, vo, oo, mo
):
    length = q_ref.shape[0]
    tile = min(TILE, length)
    cosine, sine = cos_ref[...], sin_ref[...]
    queries = turn(q_ref[...], cosine, sine).astype(bf16)
    keys = turn(k_ref[...], cosine, sine).astype(bf16)
    values = v_ref[...].astype(bf16)
    qo[...] = queries
    ko[...] = keys
    vo[...] = values
    first = pl.program_id(0) == 0
    for i in range(length // tile):
        at = slice(i * tile, (i + 1) * tile)
        scores = dot_t(queries[at], keys) * score_scale + score_bias
        visible = row_ref[...] <= col_ref[at, :]
        weights = jnp.where(visible, jax.nn.sigmoid(scores), 0.0)
        oo[at, :] = dot(weights.astype(bf16), values).astype(bf16)
        mass = jnp.sum(weights, axis=1, keepdims=True) * (1.0 / heads_all)
        mass = jnp.broadcast_to(mass, (tile, LANES))
        mo[at, :] = jnp.where(first, mass, mo[at, :] + mass)


def attend(qkv, cosine, sine, pos_col, pos_row, heads, heads_all):
    length = qkv.shape[0]
    part = lambda j: pl.BlockSpec((length, HD), lambda i, j=j: (0, i + j * heads))
    out = jax.ShapeDtypeStruct((length, heads * HD), bf16)
    return call(
        functools.partial(attend_kernel, heads_all),
        heads,
        (qkv, qkv, qkv, cosine, sine, pos_col, pos_row),
        [part(0), part(1), part(2)]
        + [whole(a.shape) for a in (cosine, sine, pos_col, pos_row)],
        [out] * 4 + [jax.ShapeDtypeStruct((length, LANES), f32)],
        [part(0)] * 4 + [pl.BlockSpec((length, LANES), lambda i: (0, 0))],
        4 * heads * length * length * HD,
    )


def halves(length, cols):
    tile = min(TILE, length // 2)
    count = length // 2 // tile
    shape = jax.ShapeDtypeStruct((length // 2, cols), bf16)
    return tile, 2 * count, [shape] * 2, pair_specs(length, cols, tile)


def pair_specs(length, cols, tile):
    count = length // 2 // tile
    return [
        pl.BlockSpec((tile, cols), lambda i, *_: (jnp.minimum(i, count - 1), 0)),
        pl.BlockSpec((tile, cols), lambda i, *_: (jnp.maximum(i - count, 0), 0)),
    ]


def either(pair):
    first = pl.program_id(0) < pl.num_programs(0) // 2
    return jnp.where(first, pair[0][...], pair[1][...])


def store_half(value, outs):
    first = pl.program_id(0) < pl.num_programs(0) // 2

    @pl.when(first)
    def _():
        outs[0][...] = value

    @pl.when(jnp.logical_not(first))
    def _():
        outs[1][...] = value


def project_kernel(o_ref, m_ref, w_ref, *outs):
    value = dot_t(o_ref[...], w_ref[...]).astype(bf16)
    store_half(jnp.concatenate([value, m_ref[...].astype(bf16)], axis=1), outs)


def project(attended, mass, w_qko):
    length, cols = attended.shape
    width = w_qko.shape[0]
    tile, steps, outs, specs = halves(length, width + LANES)
    return call(
        project_kernel,
        steps,
        (attended, mass, w_qko),
        [rows_of(tile, cols), rows_of(tile, LANES), columns(w_qko, 2, cols)],
        outs,
        specs,
        2 * length * cols * width,
    )


def enter_kernel(a_ref, b_ref, gain_ref, wq_ref, wk_ref, wv_ref, qkv_ref, n_ref):
    rows = either((a_ref, b_ref)).astype(f32)
    normed = (rows * norm_scale(rows) * gain_ref[...]).astype(bf16)
    n_ref[...] = normed
    cols = wq_ref.shape[1]
    for i, ref in enumerate((wq_ref, wk_ref, wv_ref)):
        qkv_ref[:, i * cols : (i + 1) * cols] = dot(normed, ref[...])


def enter(x_pair, gain, w_qko, w_v):
    length, width = 2 * x_pair[0].shape[0], x_pair[0].shape[1]
    one = w_v.shape[1]
    cols = 3 * one
    tile = min(TILE, length // 2)
    return call(
        enter_kernel,
        length // tile,
        (*x_pair, gain, w_qko, w_qko, w_v),
        pair_specs(length, width, tile)
        + [whole(gain.shape), columns(w_qko, 0, one), columns(w_qko, 1, one), whole(w_v.shape)],
        [
            jax.ShapeDtypeStruct((length, cols), f32),
            jax.ShapeDtypeStruct((length, width), bf16),
        ],
        [rows_of(tile, cols), rows_of(tile, width)],
        2 * length * width * cols,
    )


def ffn_kernel(na_ref, nb_ref, da_ref, db_ref, w_ref, act_ref, back_ref):
    cols = act_ref.shape[1]
    gated = dot(either((na_ref, nb_ref)), w_ref[:, : 2 * cols])
    grad_act = dot(either((da_ref, db_ref)), w_ref[:, 2 * cols :])
    gate, up = gated[:, :cols], gated[:, cols:]
    sig = jax.nn.sigmoid(gate)
    silu = gate * sig
    act_ref[...] = (silu * up).astype(bf16)
    back_ref[:, :cols] = (grad_act * up * sig * (1.0 + gate * (1.0 - sig))).astype(bf16)
    back_ref[:, cols:] = (grad_act * silu).astype(bf16)


def ffn(n_pair, d_pair, w):
    length, width = 2 * n_pair[0].shape[0], n_pair[0].shape[1]
    cols = w.shape[1] // 3
    tile = min(2 * TILE, length // 2)
    return call(
        ffn_kernel,
        length // tile,
        (*n_pair, *d_pair, w),
        pair_specs(length, width, tile) * 2 + [whole(w.shape)],
        [
            jax.ShapeDtypeStruct((length, cols), bf16),
            jax.ShapeDtypeStruct((length, 2 * cols), bf16),
        ],
        [rows_of(tile, cols), rows_of(tile, 2 * cols)],
        6 * length * width * cols,
    )


def cols_of(length, tile):
    return pl.BlockSpec((length, tile), lambda i, *_: (0, i))


def t_dot_pair(pair, right):
    half = pair[0].shape[0]
    return t_dot(pair[0][...], right[:half, :]) + t_dot(pair[1][...], right[half:, :])


def ffn_sums_kernel(na_ref, nb_ref, da_ref, db_ref, act_ref, back_ref, w_ref, sum_ref, gain_ref):
    cols = act_ref.shape[1]
    gated = t_dot_pair((na_ref, nb_ref), back_ref)
    sum_ref[:, : 2 * cols] = gated.astype(bf16)
    sum_ref[:, 2 * cols :] = t_dot_pair((da_ref, db_ref), act_ref).astype(bf16)
    gain = jnp.sum(gated * w_ref[:, : 2 * cols].astype(f32), axis=1, keepdims=True)
    gain_ref[...] = jnp.broadcast_to(gain, gain_ref.shape)


def ffn_sums(n_pair, d_pair, act, back, w):
    half, width = n_pair[0].shape
    cols = act.shape[1]
    tile = min(2 * TILE, width)
    return call(
        ffn_sums_kernel,
        width // tile,
        (*n_pair, *d_pair, act, back, w),
        [cols_of(half, tile)] * 4
        + [whole(act.shape), whole(back.shape), rows_of(tile, 3 * cols)],
        [
            jax.ShapeDtypeStruct((width, 3 * cols), bf16),
            jax.ShapeDtypeStruct((width, LANES), f32),
        ],
        [rows_of(tile, 3 * cols), rows_of(tile, LANES)],
        12 * half * width * cols,
    )


def branch_kernel(a_ref, b_ref, w_ref, out_ref):
    out_ref[...] = dot(either((a_ref, b_ref)), w_ref[...]).astype(bf16)


def branch_back(pair, w_qko):
    length, width = 2 * pair[0].shape[0], pair[0].shape[1]
    cols = w_qko.shape[1] // 3
    tile = min(TILE, length // 2)
    return call(
        branch_kernel,
        length // tile,
        (*pair, w_qko),
        pair_specs(length, width, tile) + [columns(w_qko, 2, cols)],
        [jax.ShapeDtypeStruct((length, cols), bf16)],
        [rows_of(tile, cols)],
        2 * length * width * cols,
    )


def branch_sums_kernel(a_ref, b_ref, o_ref, sum_ref):
    sum_ref[...] = t_dot_pair((a_ref, b_ref), o_ref).astype(bf16)


def branch_sums(pair, attended):
    half, width = pair[0].shape
    cols = attended.shape[1]
    tile = min(2 * TILE, width)
    return call(
        branch_sums_kernel,
        width // tile,
        (*pair, attended),
        [cols_of(half, tile)] * 2 + [whole(attended.shape)],
        [jax.ShapeDtypeStruct((width, cols), bf16)],
        [rows_of(tile, cols)],
        4 * half * width * cols,
    )


def back_kernel(count, first, *refs):
    lefts, rights, outs = refs[:count], refs[count : 2 * count], refs[2 * count :]
    total = 0.0
    for left, right in zip(lefts, rights):
        cols = left.shape[1]
        total = total + dot_t(left[...], right[:, first : first + cols])
    store_half(total.astype(bf16), outs)


def enter_back(lefts, w_qko, w_v):
    length, cols = lefts[0].shape
    width = w_v.shape[0]
    tile, steps, outs, specs = halves(length, width)
    return call(
        functools.partial(back_kernel, 3, 0),
        steps,
        (*lefts, w_qko, w_qko, w_v),
        [rows_of(tile, cols)] * 3
        + [columns(w_qko, 0, cols), columns(w_qko, 1, cols), whole(w_v.shape)],
        outs,
        specs,
        6 * length * width * cols,
    )


def back(lefts, rights, first=0):
    length = lefts[0].shape[0]
    width = rights[0].shape[0]
    tile, steps, outs, specs = halves(length, width)
    return call(
        functools.partial(back_kernel, len(lefts), first),
        steps,
        (*lefts, *rights),
        [rows_of(tile, a.shape[1]) for a in lefts] + [whole(a.shape) for a in rights],
        outs,
        specs,
        2 * length * width * sum(a.shape[1] for a in lefts),
    )


def attend_back_kernel(q_ref, k_ref, v_ref, g_ref, cos_ref, sin_ref, col_ref, row_ref, dq, dk, dv):
    length = q_ref.shape[0]
    tile = min(TILE, length)
    cosine, sine = cos_ref[...], -sin_ref[...]
    queries, keys, values, grads = q_ref[...], k_ref[...], v_ref[...], g_ref[...]
    grad_keys = grad_values = 0.0
    for i in range(length // tile):
        at = slice(i * tile, (i + 1) * tile)
        scores = dot_t(keys, queries[at]) * score_scale + score_bias
        visible = col_ref[...] <= row_ref[:, at]
        weights = jnp.where(visible, jax.nn.sigmoid(scores), 0.0)
        grad_weights = dot_t(values, grads[at])
        grad_scores = (grad_weights * weights * (1.0 - weights)).astype(bf16)
        grad_values = grad_values + dot(weights.astype(bf16), grads[at])
        grad_keys = grad_keys + dot(grad_scores, queries[at])
        grad_query = t_dot(grad_scores, keys) * score_scale
        dq[at, :] = turn(grad_query, cosine[at], sine[at]).astype(bf16)
    dk[...] = turn(grad_keys * score_scale, cosine, sine).astype(bf16)
    dv[...] = grad_values.astype(bf16)


def attend_back(queries, keys, values, grads, cosine, sine, pos_col, pos_row):
    length, cols = queries.shape
    heads = cols // HD
    part = pl.BlockSpec((length, HD), lambda i: (0, i))
    out = jax.ShapeDtypeStruct((length, cols), bf16)
    return call(
        attend_back_kernel,
        heads,
        (queries, keys, values, grads, cosine, sine, pos_col, pos_row),
        [part] * 4 + [whole(a.shape) for a in (cosine, sine, pos_col, pos_row)],
        [out] * 3,
        [part] * 3,
        10 * heads * length * length * HD,
    )


def qkv_sums_kernel(n_ref, dq, dk, dv, wq_ref, wk_ref, wv_ref, other_ref, out_ref):
    cols = dq.shape[1]
    gain = 0.0
    for i, (ref, w) in enumerate(((dq, wq_ref), (dk, wk_ref), (dv, wv_ref))):
        part = t_dot(n_ref[...], ref[...])
        out_ref[:, i * cols : (i + 1) * cols] = part.astype(bf16)
        gain = gain + jnp.sum(part * w[...].astype(f32), axis=1, keepdims=True)
    lane = lax.broadcasted_iota(jnp.int32, other_ref.shape, 1)
    gains = jnp.where(lane == 0, gain, other_ref[...])
    out_ref[:, 3 * cols :] = gains.astype(bf16)


def qkv_sums(normed, dq, dk, dv, w_qko, w_v, other):
    length, width = normed.shape
    cols = dq.shape[1]
    tile = min(2 * TILE, width)
    return call(
        qkv_sums_kernel,
        width // tile,
        (normed, dq, dk, dv, w_qko, w_qko, w_v, other),
        [cols_of(length, tile)]
        + [whole(a.shape) for a in (dq, dk, dv)]
        + [pl.BlockSpec((tile, cols), lambda i, at=at: (i, at)) for at in (0, 1, 0)]
        + [rows_of(tile, LANES)],
        [jax.ShapeDtypeStruct((width, 3 * cols + LANES), bf16)],
        [rows_of(tile, 3 * cols + LANES)],
        6 * length * width * cols,
    )


def unpack_kernel(count, parts, *refs):
    ins, outs = refs[:count], refs[count:]
    cols = outs[0].shape[1] // count
    for c, ref in enumerate(ins):
        for i in range(parts):
            outs[i][:, c * cols : (c + 1) * cols] = ref[0, :, i * cols : (i + 1) * cols].astype(f32)
    for i, out in enumerate(outs[parts:]):
        step = pl.program_id(0)
        part = ref[0, :, parts * cols :].astype(f32)
        out[...] = jnp.where(step == 0, part, out[...] + part)


def unpack(blocks, parts, extra=False):
    ns, rows, cols = blocks[0].shape
    cols = (cols - LANES * extra) // parts
    outs = [jax.ShapeDtypeStruct((rows, ns * len(blocks) * cols), f32)] * parts
    specs = [pl.BlockSpec((rows, len(blocks) * cols), lambda i: (0, i))] * parts
    if extra:
        outs = outs + [jax.ShapeDtypeStruct((rows, LANES), f32)]
        specs = specs + [pl.BlockSpec((rows, LANES), lambda i: (0, 0))]
    return call(
        functools.partial(unpack_kernel, len(blocks), parts),
        ns,
        tuple(blocks),
        [pl.BlockSpec((1,) + a.shape[1:], lambda i: (i, 0, 0)) for a in blocks],
        outs,
        specs,
        0,
    )


def swap_bit(block, bit, size):
    return lax.ppermute(block, "seq", [(i, i ^ bit) for i in range(size)])


def link_bits(size):
    bits = []
    bit = 2
    while bit < size:
        bits.append(bit)
        bit *= 2
    return bits


def orders(size):
    bits = link_bits(size)
    found = []
    for run in (bits, bits[::-1]):
        order = [0]
        for bit in run:
            order += [k ^ bit for k in order]
        found.append(order)
    return found


def swap_side(block):
    return lax.ppermute(block, "side", [(0, 1), (1, 0)])


def exchange(moves, waits=()):
    blocks = lax.optimization_barrier([b for b, _ in moves])
    got = [f(b) for (_, f), b in zip(moves, blocks)]
    got, values = lax.optimization_barrier((got, [box[i] for box, i in waits]))
    for (box, i), value in zip(waits, values):
        box[i] = value
    return got


def along(bit):
    return functools.partial(swap_bit, bit=bit, size=lax.axis_size("seq"))


def gather_steps(held):
    bits = link_bits(lax.axis_size("seq"))
    for pair in zip(bits, bits[::-1]):
        got = yield [(block, along(bit)) for block, bit in zip(held, pair)]
        held = [jnp.concatenate(pieces, axis=0) for pieces in zip(held, got)]
    side = jnp.concatenate(held, axis=0)
    (got,) = yield [(side, along(1))]
    return side, got


def scatter_steps(keep, away):
    bits = link_bits(lax.axis_size("seq"))
    (got,) = yield [(away, along(1))]
    length = keep.shape[0] // 2
    terms = [[t[i * length : (i + 1) * length] for t in (keep, got)] for i in range(2)]

    def total(parts, start, stop):
        return sum(t[start:stop].astype(f32) for t in parts)

    for pair in zip(bits[::-1], bits):
        sent = [total(parts, length // 2, length).astype(bf16) for parts in terms]
        got = yield [(block, along(bit)) for block, bit in zip(sent, pair)]
        length //= 2
        for parts, block in zip(terms, got):
            parts.append(block)
    return [total(parts, 0, length) for parts in terms]


def gather_one(own):
    half = own.shape[0] // 2
    return (yield from gather_steps([own[:half], own[half:]]))


def scatter_one(pair):
    blocks = yield from scatter_steps(*pair)
    return jnp.concatenate(blocks, axis=0)


def gather_two(own):
    (got,) = yield [(own, swap_side)]
    return (yield from gather_steps([own, got]))


def scatter_two(pair):
    mine, other = yield from scatter_steps(*pair)
    (got,) = yield [(other.astype(bf16), swap_side)]
    return mine + got.astype(f32)


class Ride:
    def __init__(self, steps):
        self.steps = steps
        self.result = None
        self.feed(None)

    def feed(self, got):
        try:
            self.moves = self.steps.send(got)
        except StopIteration as end:
            self.moves, self.result = None, end.value


def run(steps, riders=(), waits=()):
    main = Ride(steps)
    waits = list(waits)
    while main.moves is not None:
        active = [main] + [rider for rider in riders if rider.moves is not None]
        got = exchange(
            [move for ride in active for move in ride.moves], waits.pop(0) if waits else ()
        )
        for ride in active:
            part, got = got[: len(ride.moves)], got[len(ride.moves) :]
            ride.feed(part)
    return main.result


def body(
    tokens,
    positions,
    gain_attn,
    query_weight,
    key_weight,
    value_weight,
    out_weight,
    gain_ffn,
    gate_weight,
    up_weight,
    down_weight,
    cotangent,
):
    ns = lax.axis_size("seq")
    nb = lax.axis_size("pair") * lax.axis_size("side")
    batch = ("pair", "side")
    near = ("side", "seq")
    rows, width = query_weight.shape
    hidden = gate_weight.shape[1]
    head_cols = width // ns
    heads = head_cols // HD
    ffn_cols = hidden // (2 * ns * CHUNKS)
    own = tokens.shape[1]

    def swap(blocks, axes="seq"):
        return lax.all_to_all(blocks, axes, split_axis=0, concat_axis=0, tiled=True)

    def gather_z(block, axes=batch):
        return lax.all_gather(block, axes, axis=0, tiled=True)

    def scatter_z(full, axes=batch):
        return lax.psum_scatter(full, axes, scatter_dimension=0, tiled=True)

    low_gains = [gain_attn.astype(bf16), gain_ffn.astype(bf16)]
    gain_cols = jnp.pad(jnp.stack(low_gains, axis=1), ((0, 0), (0, LANES - 2)))
    w_v = gather_z(jnp.concatenate([value_weight.astype(bf16), gain_cols], axis=1))

    place = positions[0]
    marks = jnp.stack([place // 128, place % 128]).astype(bf16)
    marks = jnp.pad(marks.reshape(2, -1, LANES)[:, 0], ((0, rows - 2), (0, 0)))
    attn_blocks = pack(
        (query_weight, key_weight, out_weight.T.astype(bf16)),
        [[(m, 0, 1) for m in range(3)]],
        ns,
        marks,
    )
    attn_blocks = swap(attn_blocks)
    plans = [[(m, c, CHUNKS) for m in range(3)] for c in range(CHUNKS)]
    ffn_blocks = list(pack((gate_weight, up_weight, down_weight.T.astype(bf16)), plans, 2 * ns))
    x_own, attn_blocks = lax.optimization_barrier((tokens[0], attn_blocks))
    x_all = run(gather_one(x_own))
    w_v = w_v.reshape(nb, rows, -1)
    spread = jnp.broadcast_to(w_v[None, :, :, width:], (ns, nb, rows, LANES))
    w_v = w_v[:, :, :width].reshape(nb, rows, ns, head_cols).transpose(2, 0, 1, 3)
    w_v = swap(jnp.concatenate([w_v, spread], axis=3))
    w_v = w_v.transpose(1, 0, 2, 3).reshape(width, -1)
    gain_one = w_v[:, head_cols].astype(f32)
    gain_two = w_v[:, head_cols + 1].astype(f32)
    w_v = w_v[:, :head_cols]

    around = jnp.array([[[k ^ core for k in order] for order in orders(ns)] for core in range(2)])
    around = lax.axis_index("seq") ^ around.astype(jnp.int32)
    place = attn_blocks[:, :2, -LANES:].astype(f32).astype(jnp.int32)
    place = (place[:, 0] * 128 + place[:, 1]).reshape(ns, 2, own // 2)
    place = jnp.stack([jnp.take(place[:, i], around[:, i], axis=0) for i in range(2)], axis=1)
    place = place.reshape(-1)
    half_size = HD // 2
    frequency = jnp.exp(jnp.arange(half_size).astype(f32) * (-2.0 * math.log(rope_base) / HD))
    angles = place.astype(f32)[:, None] * frequency[None, :]
    cosine, sine = jnp.cos(angles), jnp.sin(angles)
    cosine = jnp.concatenate([cosine, cosine], axis=1)
    sine = jnp.concatenate([-sine, sine], axis=1)
    pos_col, pos_row = place[:, None], place[None, :]

    attn_blocks = attn_blocks.reshape(ns * rows, -1)
    w_qko = gather_z(attn_blocks[:, : 3 * head_cols])
    (w_qko, w_v, gain_one, x_all, cosine, sine, pos_col, pos_row, ffn_blocks[0]) = (
        lax.optimization_barrier(
            (w_qko, w_v, gain_one, x_all, cosine, sine, pos_col, pos_row, ffn_blocks[0])
        )
    )
    ffn_blocks[0] = swap(ffn_blocks[0], near).reshape(2 * ns * rows, -1)

    qkv, normed = enter(x_all, gain_one[None], w_qko, w_v)
    queries, keys, values, attended, mass = attend(
        qkv, cosine, sine, pos_col, pos_row, heads, width // HD
    )
    attended, ffn_blocks = lax.optimization_barrier((attended, ffn_blocks))
    ffn_blocks[0], ffn_blocks[1] = lax.optimization_barrier((ffn_blocks[0], ffn_blocks[1]))
    ffn_blocks[1] = swap(ffn_blocks[1], near).reshape(2 * ns * rows, -1)
    w_ffn = [gather_z(block, "pair") for block in ffn_blocks]
    dy_ride = Ride(gather_two(cotangent[0]))
    attn_own = run(
        scatter_one(project(attended, mass, w_qko)), [dy_ride], [[], [(w_ffn, 0)]]
    )
    attn_mass = attn_own[:, width]
    x_own_f = x_own.astype(f32)
    hidden_own = x_own_f + attn_own[:, :width]
    scale_two = norm_scale(hidden_own)
    unit_two = hidden_own * scale_two
    normed_ffn = run(
        gather_two((unit_two * gain_two).astype(bf16)),
        [dy_ride],
        [[], [], [(w_ffn, 1)]],
    )
    dy_all = dy_ride.result

    acts, backs, sums, gain_sums = [], [], [], []
    for c in range(CHUNKS):
        act, grads = ffn(normed_ffn, dy_all, w_ffn[c])
        if c + 1 == CHUNKS:
            grads_pair = back(backs + [grads], w_ffn)
            act, grads_pair = lax.optimization_barrier((act, grads_pair))
        part, gains = ffn_sums(normed_ffn, dy_all, act, grads, w_ffn[c])
        if c + 1 < CHUNKS:
            act, grads, part, w_ffn[c + 1] = lax.optimization_barrier(
                (act, grads, part, w_ffn[c + 1])
            )
        acts.append(act)
        backs.append(grads)
        sums.append(scatter_z(part, "pair"))
        gain_sums.append(gains)
    gain_sums = sum(gain_sums)
    grad_normed_two = run(scatter_two(grads_pair), (), [[], [], [(sums, 0)]])
    grad_hidden = cotangent[0].astype(f32) + norm_back(
        grad_normed_two, unit_two, scale_two, gain_two
    )

    def home(part, axes="seq"):
        return swap(part.reshape(lax.axis_size(axes), rows, -1), axes)

    branch = run(gather_one(grad_hidden.astype(bf16)), (), [[], [(sums, 1)]])
    out_sum = branch_sums(branch, attended)
    branch, out_sum = lax.optimization_barrier((branch, out_sum))
    out_sum = scatter_z(out_sum)
    grad_heads = branch_back(branch, w_qko)
    dq, dk, dv = attend_back(queries, keys, values, grad_heads, cosine, sine, pos_col, pos_row)
    ffn_sum = [home(sums[0], near)]
    dq, ffn_sum = lax.optimization_barrier((dq, ffn_sum))
    qkv_local = qkv_sums(normed, dq, dk, dv, w_qko, w_v, gain_sums)
    dq, dk, dv, qkv_local = lax.optimization_barrier((dq, dk, dv, qkv_local))
    qkv_sum = scatter_z(qkv_local)
    part = enter_back([dq, dk, dv], w_qko, w_v)
    part, acts = lax.optimization_barrier((part, acts))
    out_ride = Ride(scatter_two(back(acts, w_ffn, 2 * ffn_cols)))
    grad_normed = run(scatter_one(part), [out_ride])
    (got,) = exchange(out_ride.moves)
    out_ride.feed([got])
    layer_out = (hidden_own + out_ride.result).astype(bf16)
    ffn_sum.append(home(sums[1], near))
    scale_one = norm_scale(x_own_f)
    input_grad = (
        grad_hidden + norm_back(grad_normed, x_own_f * scale_one, scale_one, gain_one)
    ).astype(bf16)

    gate_grad, up_grad, down_grad = unpack(ffn_sum, 3)
    out_grad = unpack([home(out_sum)], 1).T
    down_grad = down_grad.T
    gate_grad, up_grad, down_grad, out_grad, qkv_sum = lax.optimization_barrier(
        (gate_grad, up_grad, down_grad, out_grad, qkv_sum)
    )
    query_grad, key_grad, value_grad, gains = unpack([home(qkv_sum)], 3, True)
    return (
        layer_out[None],
        input_grad[None],
        attn_mass[None],
        gains[:, 0] / low_gains[0].astype(f32),
        query_grad,
        key_grad,
        value_grad,
        out_grad,
        gains[:, 1] / low_gains[1].astype(f32),
        gate_grad,
        up_grad,
        down_grad,
    )


def solution(mesh):
    nb, ns = mesh.shape["batch"], mesh.shape["seq"]
    mesh = jax.sharding.Mesh(mesh.devices.reshape(nb // 2, 2, ns), ("pair", "side", "seq"))
    batch = ("pair", "side")
    both = ("pair", "side", "seq")
    token_spec = P(batch, "seq", None)
    row_spec = P(both, None)
    col_spec = P(None, both)
    return jax.shard_map(
        body,
        mesh=mesh,
        in_specs=(
            token_spec,
            P(batch, "seq"),
            P(both),
            row_spec,
            row_spec,
            row_spec,
            col_spec,
            P(both),
            row_spec,
            row_spec,
            col_spec,
            token_spec,
        ),
        out_specs=(
            token_spec,
            token_spec,
            P(batch, "seq"),
            P(both),
            row_spec,
            row_spec,
            row_spec,
            col_spec,
            P(both),
            row_spec,
            row_spec,
            col_spec,
        ),
        check_vma=False,
    )
```

```python
import functools
import math

import jax
import jax.numpy as jnp
from jax import lax
from jax.experimental import pallas as pl
from jax.experimental.pallas import tpu as pltpu
from jax.sharding import PartitionSpec as P

HD = 128
LANES = 128
epsilon = 1e-05
rope_base = 10000.0
score_bias = -math.log(4096.0)
score_scale = 1.0 / math.sqrt(HD)
f32 = jnp.float32
bf16 = jnp.bfloat16
CHUNKS = 2
TILE = 256
MIB = 1 << 20


def dot(left, right):
    return jnp.dot(left, right, preferred_element_type=f32)


def dot_t(left, right):
    return lax.dot_general(left, right, (((1,), (1,)), ((), ())), preferred_element_type=f32)


def t_dot(left, right):
    return lax.dot_general(left, right, (((0,), (0,)), ((), ())), preferred_element_type=f32)


def norm_scale(values):
    return lax.rsqrt(jnp.mean(values * values, axis=-1, keepdims=True) + epsilon)


def norm_back(grad_normed, unit_rows, scale_rows, gain_vec):
    grad_unit = grad_normed * gain_vec
    return scale_rows * (
        grad_unit - unit_rows * jnp.mean(grad_unit * unit_rows, axis=-1, keepdims=True)
    )


def columns(array, at, cols):
    return pl.BlockSpec((array.shape[0], cols), lambda *_: (0, at), pipeline_mode=pl.Buffered(1))


def whole(shape):
    zeros = (0,) * len(shape)
    return pl.BlockSpec(shape, lambda *_: zeros, pipeline_mode=pl.Buffered(1))


def rows_of(tile, cols):
    return pl.BlockSpec((tile, cols), lambda i, *_: (i, 0))


def call(kernel, steps, ins, in_specs, outs, out_specs, flops, vmem=60, scalars=0):
    size = sum(math.prod(a.shape) * a.dtype.itemsize for a in (*ins, *outs))
    result = pl.pallas_call(
        kernel,
        grid_spec=pltpu.PrefetchScalarGridSpec(
            num_scalar_prefetch=scalars,
            grid=(steps,),
            in_specs=in_specs,
            out_specs=out_specs,
        ),
        out_shape=outs,
        compiler_params=pltpu.CompilerParams(
            dimension_semantics=("arbitrary",), vmem_limit_bytes=vmem * MIB
        ),
        cost_estimate=pl.CostEstimate(flops=flops, bytes_accessed=size, transcendentals=0),
    )(*ins)
    return result[0] if len(outs) == 1 else result


def pack_kernel(plans, *refs):
    ins, outs = refs[: -len(plans)], refs[-len(plans) :]
    for plan, out_ref in zip(plans, outs):
        at = 0
        for m, part, parts in plan:
            cols = ins[m].shape[1] // parts
            value = ins[m][:, part * cols : (part + 1) * cols]
            out_ref[0, :, at : at + cols] = value.astype(bf16)
            at += cols


def pack(arrays, plans, ns, marks=None):
    rows = arrays[0].shape[0]
    specs = [pl.BlockSpec((rows, a.shape[1] // ns), lambda i: (0, i)) for a in arrays]
    widths = [a.shape[1] // ns for a in arrays]
    if marks is not None:
        plans = [plan + [(len(arrays), 0, 1)] for plan in plans]
        arrays = arrays + (marks,)
        specs.append(whole(marks.shape))
        widths.append(marks.shape[1])
    cols = [sum(widths[m] // parts for m, _, parts in plan) for plan in plans]
    return call(
        functools.partial(pack_kernel, plans),
        ns,
        arrays,
        specs,
        [jax.ShapeDtypeStruct((ns, rows, n), bf16) for n in cols],
        [pl.BlockSpec((1, rows, n), lambda i: (i, 0, 0)) for n in cols],
        0,
    )


def turn(values, cosine, sine):
    return values * cosine + pltpu.roll(values, HD // 2, 1) * sine


def halves(length, cols):
    tile = min(TILE, length // 2)
    count = length // 2 // tile
    shape = jax.ShapeDtypeStruct((length // 2, cols), bf16)
    return tile, 2 * count, [shape] * 2, pair_specs(length, cols, tile)


def pair_specs(length, cols, tile):
    count = length // 2 // tile
    return [
        pl.BlockSpec((tile, cols), lambda i, *_: (jnp.minimum(i, count - 1), 0)),
        pl.BlockSpec((tile, cols), lambda i, *_: (jnp.maximum(i - count, 0), 0)),
    ]


def either(pair):
    first = pl.program_id(0) < pl.num_programs(0) // 2
    return jnp.where(first, pair[0][...], pair[1][...])


def store_half(value, outs):
    first = pl.program_id(0) < pl.num_programs(0) // 2

    @pl.when(first)
    def _():
        outs[0][...] = value

    @pl.when(jnp.logical_not(first))
    def _():
        outs[1][...] = value


def later(i, first, count):
    return jnp.clip(i - first, 0, count - 1)


def front_kernel(
    heads_all, steps, xa, xb, gain_ref, wq, wk, wv, wo, cos, sin, col, row, *refs
):
    n_ref, qo, ko, vo, oo, keep, away, qkv, mass = refs
    i = pl.program_id(0)
    tile = n_ref.shape[0]
    cols = wq.shape[1]

    @pl.when(i < steps)
    def _():
        rows = jnp.where(i < steps // 2, xa[...], xb[...]).astype(f32)
        normed = (rows * norm_scale(rows) * gain_ref[...]).astype(bf16)
        n_ref[...] = normed
        at = pl.ds(pl.multiple_of(i * tile, tile), tile)
        for j, w in enumerate((wq, wk, wv)):
            qkv[at, j * cols : (j + 1) * cols] = dot(normed, w[...])

    @pl.when(i == steps - 1)
    def _():
        cosine, sine = cos[...], sin[...]
        for h in range(cols // HD):
            head = slice(h * HD, (h + 1) * HD)
            queries = turn(qkv[:, h * HD : (h + 1) * HD], cosine, sine).astype(bf16)
            keys = turn(qkv[:, cols + h * HD : cols + (h + 1) * HD], cosine, sine).astype(bf16)
            values = qkv[:, 2 * cols + h * HD : 2 * cols + (h + 1) * HD].astype(bf16)
            qo[:, head] = queries
            ko[:, head] = keys
            vo[:, head] = values
            for j in range(steps):
                at = slice(j * tile, (j + 1) * tile)
                scores = dot_t(queries[at], keys) * score_scale + score_bias
                weights = jnp.where(row[...] <= col[at, :], jax.nn.sigmoid(scores), 0.0)
                oo[at, head] = dot(weights.astype(bf16), values).astype(bf16)
                part = jnp.sum(weights, axis=1, keepdims=True) * (1.0 / heads_all)
                part = jnp.broadcast_to(part, (tile, LANES))
                mass[at, :] = part if h == 0 else mass[at, :] + part

    def projected():
        at = pl.ds(pl.multiple_of((i - steps) * tile, tile), tile)
        value = dot_t(oo[at, :], wo[...]).astype(bf16)
        return jnp.concatenate([value, mass[at, :].astype(bf16)], axis=1)

    @pl.when((i >= steps) & (i < steps + steps // 2))
    def _():
        keep[...] = projected()

    @pl.when(i >= steps + steps // 2)
    def _():
        away[...] = projected()


def front(x_pair, gain, w_qko, w_v, cosine, sine, pos_col, pos_row, heads_all):
    length, width = 2 * x_pair[0].shape[0], x_pair[0].shape[1]
    cols = w_v.shape[1]
    tile = min(TILE, length // 2)
    steps = length // tile
    half = steps // 2
    constants = (cosine, sine, pos_col, pos_row)
    rows = jax.ShapeDtypeStruct((length, cols), bf16)
    sides = jax.ShapeDtypeStruct((length // 2, width + LANES), bf16)
    return pl.pallas_call(
        functools.partial(front_kernel, heads_all, steps),
        grid=(2 * steps,),
        in_specs=[
            pl.BlockSpec((tile, width), lambda i: (later(i, 0, half), 0)),
            pl.BlockSpec((tile, width), lambda i: (later(i, half, half), 0)),
            whole(gain.shape),
            columns(w_qko, 0, cols),
            columns(w_qko, 1, cols),
            whole(w_v.shape),
            columns(w_qko, 2, cols),
        ]
        + [whole(a.shape) for a in constants],
        out_specs=[pl.BlockSpec((tile, width), lambda i: (later(i, 0, steps), 0))]
        + [pl.BlockSpec((length, cols), lambda i: (0, 0))] * 4
        + [
            pl.BlockSpec((tile, width + LANES), lambda i: (later(i, steps, half), 0)),
            pl.BlockSpec((tile, width + LANES), lambda i: (later(i, steps + half, half), 0)),
        ],
        out_shape=[jax.ShapeDtypeStruct((length, width), bf16)] + [rows] * 4 + [sides] * 2,
        scratch_shapes=[pltpu.VMEM((length, 3 * cols), f32), pltpu.VMEM((length, LANES), f32)],
        compiler_params=pltpu.CompilerParams(
            dimension_semantics=("arbitrary",), vmem_limit_bytes=60 * MIB
        ),
        cost_estimate=pl.CostEstimate(
            flops=8 * length * width * cols,
            bytes_accessed=12 * length * width,
            transcendentals=0,
        ),
    )(*x_pair, gain, w_qko, w_qko, w_v, w_qko, *constants)


def ffn_kernel(na_ref, nb_ref, da_ref, db_ref, w_ref, act_ref, back_ref):
    cols = act_ref.shape[1]
    gated = dot(either((na_ref, nb_ref)), w_ref[:, : 2 * cols])
    grad_act = dot(either((da_ref, db_ref)), w_ref[:, 2 * cols :])
    gate, up = gated[:, :cols], gated[:, cols:]
    sig = jax.nn.sigmoid(gate)
    silu = gate * sig
    act_ref[...] = (silu * up).astype(bf16)
    back_ref[:, :cols] = (grad_act * up * sig * (1.0 + gate * (1.0 - sig))).astype(bf16)
    back_ref[:, cols:] = (grad_act * silu).astype(bf16)


def ffn(n_pair, d_pair, w):
    length, width = 2 * n_pair[0].shape[0], n_pair[0].shape[1]
    cols = w.shape[1] // 3
    tile = min(2 * TILE, length // 2)
    return call(
        ffn_kernel,
        length // tile,
        (*n_pair, *d_pair, w),
        pair_specs(length, width, tile) * 2 + [whole(w.shape)],
        [
            jax.ShapeDtypeStruct((length, cols), bf16),
            jax.ShapeDtypeStruct((length, 2 * cols), bf16),
        ],
        [rows_of(tile, cols), rows_of(tile, 2 * cols)],
        6 * length * width * cols,
    )


def cols_of(length, tile):
    return pl.BlockSpec((length, tile), lambda i, *_: (0, i))


def t_dot_pair(pair, right):
    half = pair[0].shape[0]
    return t_dot(pair[0][...], right[:half, :]) + t_dot(pair[1][...], right[half:, :])


def ffn_sums_kernel(na_ref, nb_ref, da_ref, db_ref, act_ref, back_ref, w_ref, sum_ref, gain_ref):
    cols = act_ref.shape[1]
    gated = t_dot_pair((na_ref, nb_ref), back_ref)
    sum_ref[:, : 2 * cols] = gated.astype(bf16)
    sum_ref[:, 2 * cols :] = t_dot_pair((da_ref, db_ref), act_ref).astype(bf16)
    gain = jnp.sum(gated * w_ref[:, : 2 * cols].astype(f32), axis=1, keepdims=True)
    gain_ref[...] = jnp.broadcast_to(gain, gain_ref.shape)


def ffn_sums(n_pair, d_pair, act, back, w):
    half, width = n_pair[0].shape
    cols = act.shape[1]
    tile = min(2 * TILE, width)
    return call(
        ffn_sums_kernel,
        width // tile,
        (*n_pair, *d_pair, act, back, w),
        [cols_of(half, tile)] * 4
        + [whole(act.shape), whole(back.shape), rows_of(tile, 3 * cols)],
        [
            jax.ShapeDtypeStruct((width, 3 * cols), bf16),
            jax.ShapeDtypeStruct((width, LANES), f32),
        ],
        [rows_of(tile, 3 * cols), rows_of(tile, LANES)],
        12 * half * width * cols,
    )


def branch_sums_kernel(a_ref, b_ref, o_ref, sum_ref):
    sum_ref[...] = t_dot_pair((a_ref, b_ref), o_ref).astype(bf16)


def branch_sums(pair, attended):
    half, width = pair[0].shape
    cols = attended.shape[1]
    tile = min(2 * TILE, width)
    return call(
        branch_sums_kernel,
        width // tile,
        (*pair, attended),
        [cols_of(half, tile)] * 2 + [whole(attended.shape)],
        [jax.ShapeDtypeStruct((width, cols), bf16)],
        [rows_of(tile, cols)],
        4 * half * width * cols,
    )


def back_kernel(count, first, *refs):
    lefts, rights, outs = refs[:count], refs[count : 2 * count], refs[2 * count :]
    total = 0.0
    for left, right in zip(lefts, rights):
        cols = left.shape[1]
        total = total + dot_t(left[...], right[:, first : first + cols])
    store_half(total.astype(bf16), outs)


def enter_back(lefts, w_qko, w_v):
    length, cols = lefts[0].shape
    width = w_v.shape[0]
    tile, steps, outs, specs = halves(length, width)
    return call(
        functools.partial(back_kernel, 3, 0),
        steps,
        (*lefts, w_qko, w_qko, w_v),
        [rows_of(tile, cols)] * 3
        + [columns(w_qko, 0, cols), columns(w_qko, 1, cols), whole(w_v.shape)],
        outs,
        specs,
        6 * length * width * cols,
    )


def back(lefts, rights, first=0):
    length = lefts[0].shape[0]
    width = rights[0].shape[0]
    tile, steps, outs, specs = halves(length, width)
    return call(
        functools.partial(back_kernel, len(lefts), first),
        steps,
        (*lefts, *rights),
        [rows_of(tile, a.shape[1]) for a in lefts] + [whole(a.shape) for a in rights],
        outs,
        specs,
        2 * length * width * sum(a.shape[1] for a in lefts),
    )


def rear_kernel(
    steps, ba, bb, wo, q_ref, k_ref, v_ref, cos, sin, col, row, n_ref, wq, wk, wv, g0, g1, *refs
):
    dq, dk, dv, out_ref, grads = refs
    i = pl.program_id(0)
    tile = ba.shape[0]
    cols = wo.shape[1]

    @pl.when(i < steps)
    def _():
        at = pl.ds(pl.multiple_of(i * tile, tile), tile)
        rows = jnp.where(i < steps // 2, ba[...], bb[...])
        grads[at, :] = dot(rows, wo[...]).astype(bf16)

    @pl.when(i == steps - 1)
    def _():
        cosine, sine = cos[...], -sin[...]
        for h in range(cols // HD):
            head = slice(h * HD, (h + 1) * HD)
            queries, keys, values = q_ref[:, head], k_ref[:, head], v_ref[:, head]
            gradient = grads[:, head]
            grad_keys = grad_values = 0.0
            for j in range(steps):
                at = slice(j * tile, (j + 1) * tile)
                scores = dot_t(keys, queries[at]) * score_scale + score_bias
                weights = jnp.where(col[...] <= row[:, at], jax.nn.sigmoid(scores), 0.0)
                grad_weights = dot_t(values, gradient[at])
                grad_scores = (grad_weights * weights * (1.0 - weights)).astype(bf16)
                grad_values = grad_values + dot(weights.astype(bf16), gradient[at])
                grad_keys = grad_keys + dot(grad_scores, queries[at])
                grad_query = t_dot(grad_scores, keys) * score_scale
                dq[at, head] = turn(grad_query, cosine[at], sine[at]).astype(bf16)
            dk[:, head] = turn(grad_keys * score_scale, cosine, sine).astype(bf16)
            dv[:, head] = grad_values.astype(bf16)

    @pl.when(i >= steps)
    def _():
        gain = 0.0
        for j, (ref, w) in enumerate(((dq, wq), (dk, wk), (dv, wv))):
            part = t_dot(n_ref[...], ref[...])
            out_ref[:, j * cols : (j + 1) * cols] = part.astype(bf16)
            gain = gain + jnp.sum(part * w[...].astype(f32), axis=1, keepdims=True)
        lane = lax.broadcasted_iota(jnp.int32, g0.shape, 1)
        gains = jnp.where(lane == 0, gain, g0[...] + g1[...])
        out_ref[:, 3 * cols :] = gains.astype(bf16)


def rear(pair, queries, keys, values, constants, normed, w_qko, w_v, gain_sums):
    length, width = normed.shape
    cols = w_v.shape[1]
    tile = min(TILE, length // 2)
    steps = length // tile
    half = steps // 2
    block = min(2 * TILE, width)
    blocks = width // block
    rows = jax.ShapeDtypeStruct((length, cols), bf16)
    place = lambda at: pl.BlockSpec((block, cols), lambda i: (later(i, steps, blocks), at))
    return pl.pallas_call(
        functools.partial(rear_kernel, steps),
        grid=(steps + blocks,),
        in_specs=[
            pl.BlockSpec((tile, width), lambda i: (later(i, 0, half), 0)),
            pl.BlockSpec((tile, width), lambda i: (later(i, half, half), 0)),
            columns(w_qko, 2, cols),
        ]
        + [whole(a.shape) for a in (queries, keys, values, *constants)]
        + [pl.BlockSpec((length, block), lambda i: (0, later(i, steps, blocks)))]
        + [place(0), place(1), place(0)]
        + [pl.BlockSpec((block, LANES), lambda i: (later(i, steps, blocks), 0))] * 2,
        out_specs=[pl.BlockSpec((length, cols), lambda i: (0, 0))] * 3
        + [pl.BlockSpec((block, 3 * cols + LANES), lambda i: (later(i, steps, blocks), 0))],
        out_shape=[rows] * 3 + [jax.ShapeDtypeStruct((width, 3 * cols + LANES), bf16)],
        scratch_shapes=[pltpu.VMEM((length, cols), bf16)],
        compiler_params=pltpu.CompilerParams(
            dimension_semantics=("arbitrary",), vmem_limit_bytes=60 * MIB
        ),
        cost_estimate=pl.CostEstimate(
            flops=8 * length * width * cols,
            bytes_accessed=8 * length * width,
            transcendentals=0,
        ),
    )(*pair, w_qko, queries, keys, values, *constants, normed, w_qko, w_qko, w_v, *gain_sums)


def unpack_kernel(count, parts, *refs):
    ins, outs = refs[:count], refs[count:]
    cols = outs[0].shape[1] // count
    for c, ref in enumerate(ins):
        for i in range(parts):
            outs[i][:, c * cols : (c + 1) * cols] = ref[0, :, i * cols : (i + 1) * cols].astype(f32)
    for i, out in enumerate(outs[parts:]):
        step = pl.program_id(0)
        part = ref[0, :, parts * cols :].astype(f32)
        out[...] = jnp.where(step == 0, part, out[...] + part)


def unpack(blocks, parts, extra=False):
    ns, rows, cols = blocks[0].shape
    cols = (cols - LANES * extra) // parts
    outs = [jax.ShapeDtypeStruct((rows, ns * len(blocks) * cols), f32)] * parts
    specs = [pl.BlockSpec((rows, len(blocks) * cols), lambda i: (0, i))] * parts
    if extra:
        outs = outs + [jax.ShapeDtypeStruct((rows, LANES), f32)]
        specs = specs + [pl.BlockSpec((rows, LANES), lambda i: (0, 0))]
    return call(
        functools.partial(unpack_kernel, len(blocks), parts),
        ns,
        tuple(blocks),
        [pl.BlockSpec((1,) + a.shape[1:], lambda i: (i, 0, 0)) for a in blocks],
        outs,
        specs,
        0,
    )


def swap_bit(block, bit, size):
    return lax.ppermute(block, "seq", [(i, i ^ bit) for i in range(size)])


def link_bits(size):
    bits = []
    bit = 2
    while bit < size:
        bits.append(bit)
        bit *= 2
    return bits


def orders(size):
    bits = link_bits(size)
    found = []
    for run in (bits, bits[::-1]):
        order = [0]
        for bit in run:
            order += [k ^ bit for k in order]
        found.append(order)
    return found


def swap_side(block):
    return lax.ppermute(block, "side", [(0, 1), (1, 0)])


def exchange(moves, waits=()):
    blocks = lax.optimization_barrier([b for b, _ in moves])
    got = [f(b) for (_, f), b in zip(moves, blocks)]
    got, values = lax.optimization_barrier((got, [box[i] for box, i in waits]))
    for (box, i), value in zip(waits, values):
        box[i] = value
    return got


def along(bit):
    return functools.partial(swap_bit, bit=bit, size=lax.axis_size("seq"))


def gather_steps(held):
    bits = link_bits(lax.axis_size("seq"))
    for pair in zip(bits, bits[::-1]):
        got = yield [(block, along(bit)) for block, bit in zip(held, pair)]
        held = [jnp.concatenate(pieces, axis=0) for pieces in zip(held, got)]
    side = jnp.concatenate(held, axis=0)
    (got,) = yield [(side, along(1))]
    return side, got


def scatter_steps(keep, away):
    bits = link_bits(lax.axis_size("seq"))
    (got,) = yield [(away, along(1))]
    length = keep.shape[0] // 2
    terms = [[t[i * length : (i + 1) * length] for t in (keep, got)] for i in range(2)]

    def total(parts, start, stop):
        return sum(t[start:stop].astype(f32) for t in parts)

    for pair in zip(bits[::-1], bits):
        sent = [total(parts, length // 2, length).astype(bf16) for parts in terms]
        got = yield [(block, along(bit)) for block, bit in zip(sent, pair)]
        length //= 2
        for parts, block in zip(terms, got):
            parts.append(block)
    return [total(parts, 0, length) for parts in terms]


def gather_one(own):
    half = own.shape[0] // 2
    return (yield from gather_steps([own[:half], own[half:]]))


def scatter_one(pair):
    blocks = yield from scatter_steps(*pair)
    return jnp.concatenate(blocks, axis=0)


def gather_two(own):
    (got,) = yield [(own, swap_side)]
    return (yield from gather_steps([own, got]))


def scatter_two(pair):
    mine, other = yield from scatter_steps(*pair)
    (got,) = yield [(other.astype(bf16), swap_side)]
    return mine + got.astype(f32)


class Ride:
    def __init__(self, steps):
        self.steps = steps
        self.result = None
        self.feed(None)

    def feed(self, got):
        try:
            self.moves = self.steps.send(got)
        except StopIteration as end:
            self.moves, self.result = None, end.value


def run(steps, riders=(), waits=(), then=(), late=0):
    main = steps if isinstance(steps, Ride) else Ride(steps)
    waits, then = list(waits), list(then)
    while main.moves is not None:
        active = [main] + [rider for rider in riders if rider.moves is not None and late <= 0]
        late -= 1
        got = exchange(
            [move for ride in active for move in ride.moves], waits.pop(0) if waits else ()
        )
        for ride in active:
            part, got = got[: len(ride.moves)], got[len(ride.moves) :]
            ride.feed(part)
        if then:
            then.pop(0)()
    return main.result


def body(
    tokens,
    positions,
    gain_attn,
    query_weight,
    key_weight,
    value_weight,
    out_weight,
    gain_ffn,
    gate_weight,
    up_weight,
    down_weight,
    cotangent,
):
    ns = lax.axis_size("seq")
    nb = lax.axis_size("pair") * lax.axis_size("side")
    batch = ("pair", "side")
    near = ("side", "seq")
    rows, width = query_weight.shape
    hidden = gate_weight.shape[1]
    head_cols = width // ns
    heads = head_cols // HD
    ffn_cols = hidden // (2 * ns * CHUNKS)
    own = tokens.shape[1]

    def swap(blocks, axes="seq"):
        return lax.all_to_all(blocks, axes, split_axis=0, concat_axis=0, tiled=True)

    def gather_z(block, axes=batch):
        return lax.all_gather(block, axes, axis=0, tiled=True)

    def scatter_z(full, axes=batch):
        return lax.psum_scatter(full, axes, scatter_dimension=0, tiled=True)

    low_gains = [gain_attn.astype(bf16), gain_ffn.astype(bf16)]
    gain_cols = jnp.pad(jnp.stack(low_gains, axis=1), ((0, 0), (0, LANES - 2)))
    w_v = gather_z(jnp.concatenate([value_weight.astype(bf16), gain_cols], axis=1))

    place = positions[0]
    marks = jnp.stack([place // 128, place % 128]).astype(bf16)
    marks = jnp.pad(marks.reshape(2, -1, LANES)[:, 0], ((0, rows - 2), (0, 0)))
    attn_blocks = pack(
        (query_weight, key_weight, out_weight.T.astype(bf16)),
        [[(m, 0, 1) for m in range(3)]],
        ns,
        marks,
    )
    attn_blocks = swap(attn_blocks)
    plans = [[(m, c, CHUNKS) for m in range(3)] for c in range(CHUNKS)]
    ffn_blocks = list(pack((gate_weight, up_weight, down_weight.T.astype(bf16)), plans, 2 * ns))
    x_own, attn_blocks = lax.optimization_barrier((tokens[0], attn_blocks))
    x_ride, dy_ride = Ride(gather_one(x_own)), Ride(gather_two(cotangent[0]))
    got = exchange(x_ride.moves + dy_ride.moves)
    x_ride.feed(got[:-1])
    dy_ride.feed(got[-1:])
    x_all = run(x_ride)
    w_v = w_v.reshape(nb, rows, -1)
    spread = jnp.broadcast_to(w_v[None, :, :, width:], (ns, nb, rows, LANES))
    w_v = w_v[:, :, :width].reshape(nb, rows, ns, head_cols).transpose(2, 0, 1, 3)
    w_v = swap(jnp.concatenate([w_v, spread], axis=3))
    w_v = w_v.transpose(1, 0, 2, 3).reshape(width, -1)
    gain_one = w_v[:, head_cols].astype(f32)
    gain_two = w_v[:, head_cols + 1].astype(f32)
    w_v = w_v[:, :head_cols]

    around = jnp.array([[[k ^ core for k in order] for order in orders(ns)] for core in range(2)])
    around = lax.axis_index("seq") ^ around.astype(jnp.int32)
    place = attn_blocks[:, :2, -LANES:].astype(f32).astype(jnp.int32)
    place = (place[:, 0] * 128 + place[:, 1]).reshape(ns, 2, own // 2)
    place = jnp.stack([jnp.take(place[:, i], around[:, i], axis=0) for i in range(2)], axis=1)
    place = place.reshape(-1)
    half_size = HD // 2
    frequency = jnp.exp(jnp.arange(half_size).astype(f32) * (-2.0 * math.log(rope_base) / HD))
    angles = place.astype(f32)[:, None] * frequency[None, :]
    cosine, sine = jnp.cos(angles), jnp.sin(angles)
    cosine = jnp.concatenate([cosine, cosine], axis=1)
    sine = jnp.concatenate([-sine, sine], axis=1)
    pos_col, pos_row = place[:, None], place[None, :]

    attn_blocks = attn_blocks.reshape(ns * rows, -1)
    w_qko = gather_z(attn_blocks[:, : 3 * head_cols])
    (w_qko, w_v, gain_one, x_all, cosine, sine, pos_col, pos_row, ffn_blocks[0]) = (
        lax.optimization_barrier(
            (w_qko, w_v, gain_one, x_all, cosine, sine, pos_col, pos_row, ffn_blocks[0])
        )
    )
    ffn_blocks[0] = swap(ffn_blocks[0], near).reshape(2 * ns * rows, -1)

    constants = (cosine, sine, pos_col, pos_row)
    normed, queries, keys, values, attended, kept, away = front(
        x_all, gain_one[None], w_qko, w_v, *constants, width // HD
    )
    w_ffn = [gather_z(ffn_blocks[0], "pair")]

    def second():
        ffn_blocks[1] = swap(ffn_blocks[1], near).reshape(2 * ns * rows, -1)

    attn_own = run(
        scatter_one((kept, away)),
        [dy_ride],
        [[(ffn_blocks, 1)], [(w_ffn, 0), (ffn_blocks, 1)]],
        [second],
    )
    w_ffn.append(gather_z(ffn_blocks[1], "pair"))
    attn_mass = attn_own[:, width]
    x_own_f = x_own.astype(f32)
    hidden_own = x_own_f + attn_own[:, :width]
    scale_two = norm_scale(hidden_own)
    unit_two = hidden_own * scale_two
    normed_ffn = run(
        gather_two((unit_two * gain_two).astype(bf16)),
        [dy_ride],
        [[], [(w_ffn, 1)]],
    )
    dy_all = dy_ride.result

    acts, backs, sums, gain_sums = [], [], [], []
    for c in range(CHUNKS):
        act, grads = ffn(normed_ffn, dy_all, w_ffn[c])
        acts.append(act)
        backs.append(grads)
        if c + 1 == CHUNKS:
            break
        part, gains = ffn_sums(normed_ffn, dy_all, act, grads, w_ffn[c])
        gain_sums.append(gains)
        acts[c], backs[c], part, w_ffn[c + 1] = lax.optimization_barrier(
            (act, grads, part, w_ffn[c + 1])
        )
        sums.append(scatter_z(part, "pair"))
    grads_pair = back(backs, w_ffn)

    def home(part, axes="seq"):
        return swap(part.reshape(lax.axis_size(axes), rows, -1), axes)

    made = []

    def last_sums():
        part, gains = ffn_sums(normed_ffn, dy_all, acts[-1], backs[-1], w_ffn[-1])
        gain_sums.append(gains)
        made.append(part)

    def leave():
        sums.append(scatter_z(made[0], "pair"))

    def output():
        made.append(back(acts, w_ffn, 2 * ffn_cols))

    grad_normed_two = run(
        scatter_two(grads_pair),
        (),
        [[(acts, 1), (backs, 1)], [(made, 0)], [(sums, 0), (acts, 0)], [(made, 1)]],
        [last_sums, leave, output],
    )
    grad_hidden = cotangent[0].astype(f32) + norm_back(
        grad_normed_two, unit_two, scale_two, gain_two
    )

    ffn_sum = [home(sums[0], near)]
    out_ride = Ride(scatter_two(made[1]))
    waits = [[], [(ffn_sum, 0), (sums, 1)]]
    branch = run(gather_one(grad_hidden.astype(bf16)), [out_ride], waits, late=2)
    out_sum = branch_sums(branch, attended)
    moves = out_ride.moves
    branch, out_sum, sent = lax.optimization_barrier((branch, out_sum, [b for b, _ in moves]))
    flying = [f(b) for (_, f), b in zip(moves, sent)]
    out_sum = scatter_z(out_sum)
    dq, dk, dv, qkv_local = rear(
        branch, queries, keys, values, constants, normed, w_qko, w_v, gain_sums
    )
    ffn_sum.append(home(sums[1], near))
    dq, dk, dv, qkv_local, ffn_sum, flying, out_sum = lax.optimization_barrier(
        (dq, dk, dv, qkv_local, ffn_sum, flying, out_sum)
    )
    out_ride.feed(flying)
    qkv_sum = scatter_z(qkv_local)
    part = enter_back([dq, dk, dv], w_qko, w_v)
    grad_normed = run(scatter_one(part), [out_ride])
    while out_ride.moves is not None:
        out_ride.feed(exchange(out_ride.moves))
    layer_out = (hidden_own + out_ride.result).astype(bf16)
    scale_one = norm_scale(x_own_f)
    input_grad = (
        grad_hidden + norm_back(grad_normed, x_own_f * scale_one, scale_one, gain_one)
    ).astype(bf16)

    gate_grad, up_grad, down_grad = unpack(ffn_sum, 3)
    attn_sums = home(jnp.concatenate([out_sum, qkv_sum], axis=1))
    out_grad, query_grad, key_grad, value_grad, gains = unpack([attn_sums], 4, True)
    out_grad, down_grad = out_grad.T, down_grad.T
    return (
        layer_out[None],
        input_grad[None],
        attn_mass[None],
        gains[:, 0] / low_gains[0].astype(f32),
        query_grad,
        key_grad,
        value_grad,
        out_grad,
        gains[:, 1] / low_gains[1].astype(f32),
        gate_grad,
        up_grad,
        down_grad,
    )


def solution(mesh):
    nb, ns = mesh.shape["batch"], mesh.shape["seq"]
    mesh = jax.sharding.Mesh(mesh.devices.reshape(nb // 2, 2, ns), ("pair", "side", "seq"))
    batch = ("pair", "side")
    both = ("pair", "side", "seq")
    token_spec = P(batch, "seq", None)
    row_spec = P(both, None)
    col_spec = P(None, both)
    return jax.shard_map(
        body,
        mesh=mesh,
        in_specs=(
            token_spec,
            P(batch, "seq"),
            P(both),
            row_spec,
            row_spec,
            row_spec,
            col_spec,
            P(both),
            row_spec,
            row_spec,
            col_spec,
            token_spec,
        ),
        out_specs=(
            token_spec,
            token_spec,
            P(batch, "seq"),
            P(both),
            row_spec,
            row_spec,
            row_spec,
            col_spec,
            P(both),
            row_spec,
            row_spec,
            col_spec,
        ),
        check_vma=False,
    )
```

```python
import functools
import math

import jax
import jax.numpy as jnp
from jax import lax
from jax.experimental import pallas as pl
from jax.experimental.pallas import tpu as pltpu
from jax.sharding import PartitionSpec as P

HD = 128
LANES = 128
epsilon = 1e-05
rope_base = 10000.0
score_bias = -math.log(4096.0)
score_scale = 1.0 / math.sqrt(HD)
f32 = jnp.float32
bf16 = jnp.bfloat16
CHUNKS = 2
TILE = 256
MIB = 1 << 20


def dot(left, right):
    return jnp.dot(left, right, preferred_element_type=f32)


def dot_t(left, right):
    return lax.dot_general(left, right, (((1,), (1,)), ((), ())), preferred_element_type=f32)


def t_dot(left, right):
    return lax.dot_general(left, right, (((0,), (0,)), ((), ())), preferred_element_type=f32)


def norm_scale(values):
    return lax.rsqrt(jnp.mean(values * values, axis=-1, keepdims=True) + epsilon)


def norm_back(grad_normed, unit_rows, scale_rows, gain_vec):
    grad_unit = grad_normed * gain_vec
    return scale_rows * (
        grad_unit - unit_rows * jnp.mean(grad_unit * unit_rows, axis=-1, keepdims=True)
    )


def columns(array, at, cols):
    return pl.BlockSpec((array.shape[0], cols), lambda *_: (0, at), pipeline_mode=pl.Buffered(1))


def whole(shape):
    zeros = (0,) * len(shape)
    return pl.BlockSpec(shape, lambda *_: zeros, pipeline_mode=pl.Buffered(1))


def rows_of(tile, cols):
    return pl.BlockSpec((tile, cols), lambda i, *_: (i, 0))


def call(kernel, steps, ins, in_specs, outs, out_specs, flops, vmem=60, scalars=0):
    size = sum(math.prod(a.shape) * a.dtype.itemsize for a in (*ins, *outs))
    result = pl.pallas_call(
        kernel,
        grid_spec=pltpu.PrefetchScalarGridSpec(
            num_scalar_prefetch=scalars,
            grid=(steps,),
            in_specs=in_specs,
            out_specs=out_specs,
        ),
        out_shape=outs,
        compiler_params=pltpu.CompilerParams(
            dimension_semantics=("arbitrary",), vmem_limit_bytes=vmem * MIB
        ),
        cost_estimate=pl.CostEstimate(flops=flops, bytes_accessed=size, transcendentals=0),
    )(*ins)
    return result[0] if len(outs) == 1 else result


def pack_kernel(plans, *refs):
    ins, outs = refs[: -len(plans)], refs[-len(plans) :]
    for plan, out_ref in zip(plans, outs):
        at = 0
        for m, part, parts in plan:
            cols = ins[m].shape[1] // parts
            value = ins[m][:, part * cols : (part + 1) * cols]
            out_ref[0, :, at : at + cols] = value.astype(bf16)
            at += cols


def pack(arrays, plans, ns, marks=None):
    rows = arrays[0].shape[0]
    specs = [pl.BlockSpec((rows, a.shape[1] // ns), lambda i: (0, i)) for a in arrays]
    widths = [a.shape[1] // ns for a in arrays]
    if marks is not None:
        plans = [plan + [(len(arrays), 0, 1)] for plan in plans]
        arrays = arrays + (marks,)
        specs.append(whole(marks.shape))
        widths.append(marks.shape[1])
    cols = [sum(widths[m] // parts for m, _, parts in plan) for plan in plans]
    return call(
        functools.partial(pack_kernel, plans),
        ns,
        arrays,
        specs,
        [jax.ShapeDtypeStruct((ns, rows, n), bf16) for n in cols],
        [pl.BlockSpec((1, rows, n), lambda i: (i, 0, 0)) for n in cols],
        0,
    )


def turn(values, cosine, sine):
    return values * cosine + pltpu.roll(values, HD // 2, 1) * sine


def halves(length, cols):
    tile = min(TILE, length // 2)
    count = length // 2 // tile
    shape = jax.ShapeDtypeStruct((length // 2, cols), bf16)
    return tile, 2 * count, [shape] * 2, pair_specs(length, cols, tile)


def pair_specs(length, cols, tile):
    count = length // 2 // tile
    return [
        pl.BlockSpec((tile, cols), lambda i, *_: (jnp.minimum(i, count - 1), 0)),
        pl.BlockSpec((tile, cols), lambda i, *_: (jnp.maximum(i - count, 0), 0)),
    ]


def either(pair):
    first = pl.program_id(0) < pl.num_programs(0) // 2
    return jnp.where(first, pair[0][...], pair[1][...])


def store_half(value, outs):
    first = pl.program_id(0) < pl.num_programs(0) // 2

    @pl.when(first)
    def _():
        outs[0][...] = value

    @pl.when(jnp.logical_not(first))
    def _():
        outs[1][...] = value


def later(i, first, count):
    return jnp.clip(i - first, 0, count - 1)


def front_kernel(
    heads_all, steps, xa, xb, gain_ref, wq, wk, wv, wo, cos, sin, col, row, *refs
):
    n_ref, qo, ko, vo, oo, keep, away, qkv, mass = refs
    i = pl.program_id(0)
    tile = n_ref.shape[0]
    cols = wq.shape[1]

    @pl.when(i < steps)
    def _():
        rows = jnp.where(i < steps // 2, xa[...], xb[...]).astype(f32)
        normed = (rows * norm_scale(rows) * gain_ref[...]).astype(bf16)
        n_ref[...] = normed
        at = pl.ds(pl.multiple_of(i * tile, tile), tile)
        for j, w in enumerate((wq, wk, wv)):
            qkv[at, j * cols : (j + 1) * cols] = dot(normed, w[...])

    @pl.when(i == steps - 1)
    def _():
        cosine, sine = cos[...], sin[...]
        for h in range(cols // HD):
            head = slice(h * HD, (h + 1) * HD)
            queries = turn(qkv[:, h * HD : (h + 1) * HD], cosine, sine).astype(bf16)
            keys = turn(qkv[:, cols + h * HD : cols + (h + 1) * HD], cosine, sine).astype(bf16)
            values = qkv[:, 2 * cols + h * HD : 2 * cols + (h + 1) * HD].astype(bf16)
            qo[:, head] = queries
            ko[:, head] = keys
            vo[:, head] = values
            for j in range(steps):
                at = slice(j * tile, (j + 1) * tile)
                scores = dot_t(queries[at], keys) * score_scale + score_bias
                weights = jnp.where(row[...] <= col[at, :], jax.nn.sigmoid(scores), 0.0)
                oo[at, head] = dot(weights.astype(bf16), values).astype(bf16)
                part = jnp.sum(weights, axis=1, keepdims=True) * (1.0 / heads_all)
                part = jnp.broadcast_to(part, (tile, LANES))
                mass[at, :] = part if h == 0 else mass[at, :] + part

    def projected():
        at = pl.ds(pl.multiple_of((i - steps) * tile, tile), tile)
        value = dot_t(oo[at, :], wo[...]).astype(bf16)
        return jnp.concatenate([value, mass[at, :].astype(bf16)], axis=1)

    @pl.when((i >= steps) & (i < steps + steps // 2))
    def _():
        keep[...] = projected()

    @pl.when(i >= steps + steps // 2)
    def _():
        away[...] = projected()


def front(x_pair, gain, w_qko, w_v, cosine, sine, pos_col, pos_row, heads_all):
    length, width = 2 * x_pair[0].shape[0], x_pair[0].shape[1]
    cols = w_v.shape[1]
    tile = min(TILE, length // 2)
    steps = length // tile
    half = steps // 2
    constants = (cosine, sine, pos_col, pos_row)
    rows = jax.ShapeDtypeStruct((length, cols), bf16)
    sides = jax.ShapeDtypeStruct((length // 2, width + LANES), bf16)
    return pl.pallas_call(
        functools.partial(front_kernel, heads_all, steps),
        grid=(2 * steps,),
        in_specs=[
            pl.BlockSpec((tile, width), lambda i: (later(i, 0, half), 0)),
            pl.BlockSpec((tile, width), lambda i: (later(i, half, half), 0)),
            whole(gain.shape),
            columns(w_qko, 0, cols),
            columns(w_qko, 1, cols),
            whole(w_v.shape),
            columns(w_qko, 2, cols),
        ]
        + [whole(a.shape) for a in constants],
        out_specs=[pl.BlockSpec((tile, width), lambda i: (later(i, 0, steps), 0))]
        + [pl.BlockSpec((length, cols), lambda i: (0, 0))] * 4
        + [
            pl.BlockSpec((tile, width + LANES), lambda i: (later(i, steps, half), 0)),
            pl.BlockSpec((tile, width + LANES), lambda i: (later(i, steps + half, half), 0)),
        ],
        out_shape=[jax.ShapeDtypeStruct((length, width), bf16)] + [rows] * 4 + [sides] * 2,
        scratch_shapes=[pltpu.VMEM((length, 3 * cols), f32), pltpu.VMEM((length, LANES), f32)],
        compiler_params=pltpu.CompilerParams(
            dimension_semantics=("arbitrary",), vmem_limit_bytes=60 * MIB
        ),
        cost_estimate=pl.CostEstimate(
            flops=8 * length * width * cols,
            bytes_accessed=12 * length * width,
            transcendentals=0,
        ),
    )(*x_pair, gain, w_qko, w_qko, w_v, w_qko, *constants)


def ffn_kernel(na_ref, nb_ref, da_ref, db_ref, gu_ref, down_ref, act_ref, back_ref):
    cols = act_ref.shape[1]
    gated = dot(either((na_ref, nb_ref)), gu_ref[...])
    grad_act = dot(either((da_ref, db_ref)), down_ref[...])
    gate, up = gated[:, :cols], gated[:, cols:]
    sig = jax.nn.sigmoid(gate)
    silu = gate * sig
    act_ref[...] = (silu * up).astype(bf16)
    back_ref[:, :cols] = (grad_act * up * sig * (1.0 + gate * (1.0 - sig))).astype(bf16)
    back_ref[:, cols:] = (grad_act * silu).astype(bf16)


def ffn(n_pair, d_pair, w):
    length, width = 2 * n_pair[0].shape[0], n_pair[0].shape[1]
    cols = w.cols
    tile = min(2 * TILE, length // 2)
    return call(
        ffn_kernel,
        length // tile,
        (*n_pair, *d_pair, w.gated, w.down),
        pair_specs(length, width, tile) * 2 + w.specs(),
        [
            jax.ShapeDtypeStruct((length, cols), bf16),
            jax.ShapeDtypeStruct((length, 2 * cols), bf16),
        ],
        [rows_of(tile, cols), rows_of(tile, 2 * cols)],
        6 * length * width * cols,
    )


def cols_of(length, tile):
    return pl.BlockSpec((length, tile), lambda i, *_: (0, i))


def t_dot_pair(pair, right):
    half = pair[0].shape[0]
    return t_dot(pair[0][...], right[:half, :]) + t_dot(pair[1][...], right[half:, :])


def ffn_sums_kernel(na_ref, nb_ref, da_ref, db_ref, act_ref, back_ref, gu_ref, sum_ref, gain_ref):
    cols = act_ref.shape[1]
    gated = t_dot_pair((na_ref, nb_ref), back_ref)
    sum_ref[:, : 2 * cols] = gated.astype(bf16)
    sum_ref[:, 2 * cols :] = t_dot_pair((da_ref, db_ref), act_ref).astype(bf16)
    gain = jnp.sum(gated * gu_ref[...].astype(f32), axis=1, keepdims=True)
    gain_ref[...] = jnp.broadcast_to(gain, gain_ref.shape)


def ffn_sums(n_pair, d_pair, act, back, w):
    half, width = n_pair[0].shape
    cols = act.shape[1]
    tile = min(2 * TILE, width)
    return call(
        ffn_sums_kernel,
        width // tile,
        (*n_pair, *d_pair, act, back, w.gated),
        [cols_of(half, tile)] * 4
        + [whole(act.shape), whole(back.shape), rows_of(tile, 2 * cols)],
        [
            jax.ShapeDtypeStruct((width, 3 * cols), bf16),
            jax.ShapeDtypeStruct((width, LANES), f32),
        ],
        [rows_of(tile, 3 * cols), rows_of(tile, LANES)],
        12 * half * width * cols,
    )


def branch_sums_kernel(a_ref, b_ref, o_ref, sum_ref):
    sum_ref[...] = t_dot_pair((a_ref, b_ref), o_ref).astype(bf16)


def branch_sums(pair, attended):
    half, width = pair[0].shape
    cols = attended.shape[1]
    tile = min(2 * TILE, width)
    return call(
        branch_sums_kernel,
        width // tile,
        (*pair, attended),
        [cols_of(half, tile)] * 2 + [whole(attended.shape)],
        [jax.ShapeDtypeStruct((width, cols), bf16)],
        [rows_of(tile, cols)],
        4 * half * width * cols,
    )


def back_kernel(count, *refs):
    lefts, rights, outs = refs[:count], refs[count : 2 * count], refs[2 * count :]
    total = sum(dot_t(left[...], right[...]) for left, right in zip(lefts, rights))
    store_half(total.astype(bf16), outs)


def enter_back(lefts, w_qko, w_v):
    length, cols = lefts[0].shape
    width = w_v.shape[0]
    tile, steps, outs, specs = halves(length, width)
    return call(
        functools.partial(back_kernel, 3),
        steps,
        (*lefts, w_qko, w_qko, w_v),
        [rows_of(tile, cols)] * 3
        + [columns(w_qko, 0, cols), columns(w_qko, 1, cols), whole(w_v.shape)],
        outs,
        specs,
        6 * length * width * cols,
    )


class Chunk:
    def __init__(self, gated, down, at):
        self.gated, self.down, self.at = gated, down, at
        self.cols = down.shape[1] // (at + 1)

    def specs(self):
        return [columns(self.gated, 0, 2 * self.cols), columns(self.down, self.at, self.cols)]


def back(lefts, chunks, which):
    length = lefts[0].shape[0]
    width = chunks[0].gated.shape[0]
    tile, steps, outs, specs = halves(length, width)
    return call(
        functools.partial(back_kernel, len(lefts)),
        steps,
        (*lefts, *((w.gated, w.down)[which] for w in chunks)),
        [rows_of(tile, a.shape[1]) for a in lefts] + [w.specs()[which] for w in chunks],
        outs,
        specs,
        2 * length * width * sum(a.shape[1] for a in lefts),
    )


def rear_kernel(
    steps, ba, bb, wo, q_ref, k_ref, v_ref, cos, sin, col, row, n_ref, wq, wk, wv, g0, g1, *refs
):
    dq, dk, dv, out_ref, grads = refs
    i = pl.program_id(0)
    tile = ba.shape[0]
    cols = wo.shape[1]

    @pl.when(i < steps)
    def _():
        at = pl.ds(pl.multiple_of(i * tile, tile), tile)
        rows = jnp.where(i < steps // 2, ba[...], bb[...])
        grads[at, :] = dot(rows, wo[...]).astype(bf16)

    @pl.when(i == steps - 1)
    def _():
        cosine, sine = cos[...], -sin[...]
        for h in range(cols // HD):
            head = slice(h * HD, (h + 1) * HD)
            queries, keys, values = q_ref[:, head], k_ref[:, head], v_ref[:, head]
            gradient = grads[:, head]
            grad_keys = grad_values = 0.0
            for j in range(steps):
                at = slice(j * tile, (j + 1) * tile)
                scores = dot_t(keys, queries[at]) * score_scale + score_bias
                weights = jnp.where(col[...] <= row[:, at], jax.nn.sigmoid(scores), 0.0)
                grad_weights = dot_t(values, gradient[at])
                grad_scores = (grad_weights * weights * (1.0 - weights)).astype(bf16)
                grad_values = grad_values + dot(weights.astype(bf16), gradient[at])
                grad_keys = grad_keys + dot(grad_scores, queries[at])
                grad_query = t_dot(grad_scores, keys) * score_scale
                dq[at, head] = turn(grad_query, cosine[at], sine[at]).astype(bf16)
            dk[:, head] = turn(grad_keys * score_scale, cosine, sine).astype(bf16)
            dv[:, head] = grad_values.astype(bf16)

    @pl.when(i >= steps)
    def _():
        gain = 0.0
        for j, (ref, w) in enumerate(((dq, wq), (dk, wk), (dv, wv))):
            part = t_dot(n_ref[...], ref[...])
            out_ref[:, j * cols : (j + 1) * cols] = part.astype(bf16)
            gain = gain + jnp.sum(part * w[...].astype(f32), axis=1, keepdims=True)
        lane = lax.broadcasted_iota(jnp.int32, g0.shape, 1)
        gains = jnp.where(lane == 0, gain, g0[...] + g1[...])
        out_ref[:, 3 * cols :] = gains.astype(bf16)


def rear(pair, queries, keys, values, constants, normed, w_qko, w_v, gain_sums):
    length, width = normed.shape
    cols = w_v.shape[1]
    tile = min(TILE, length // 2)
    steps = length // tile
    half = steps // 2
    block = min(2 * TILE, width)
    blocks = width // block
    rows = jax.ShapeDtypeStruct((length, cols), bf16)
    place = lambda at: pl.BlockSpec((block, cols), lambda i: (later(i, steps, blocks), at))
    return pl.pallas_call(
        functools.partial(rear_kernel, steps),
        grid=(steps + blocks,),
        in_specs=[
            pl.BlockSpec((tile, width), lambda i: (later(i, 0, half), 0)),
            pl.BlockSpec((tile, width), lambda i: (later(i, half, half), 0)),
            columns(w_qko, 2, cols),
        ]
        + [whole(a.shape) for a in (queries, keys, values, *constants)]
        + [pl.BlockSpec((length, block), lambda i: (0, later(i, steps, blocks)))]
        + [place(0), place(1), place(0)]
        + [pl.BlockSpec((block, LANES), lambda i: (later(i, steps, blocks), 0))] * 2,
        out_specs=[pl.BlockSpec((length, cols), lambda i: (0, 0))] * 3
        + [pl.BlockSpec((block, 3 * cols + LANES), lambda i: (later(i, steps, blocks), 0))],
        out_shape=[rows] * 3 + [jax.ShapeDtypeStruct((width, 3 * cols + LANES), bf16)],
        scratch_shapes=[pltpu.VMEM((length, cols), bf16)],
        compiler_params=pltpu.CompilerParams(
            dimension_semantics=("arbitrary",), vmem_limit_bytes=60 * MIB
        ),
        cost_estimate=pl.CostEstimate(
            flops=8 * length * width * cols,
            bytes_accessed=8 * length * width,
            transcendentals=0,
        ),
    )(*pair, w_qko, queries, keys, values, *constants, normed, w_qko, w_qko, w_v, *gain_sums)


def unpack_kernel(count, parts, *refs):
    ins, outs = refs[:count], refs[count:]
    cols = outs[0].shape[1] // count
    for c, ref in enumerate(ins):
        for i in range(parts):
            outs[i][:, c * cols : (c + 1) * cols] = ref[0, :, i * cols : (i + 1) * cols].astype(f32)
    for i, out in enumerate(outs[parts:]):
        step = pl.program_id(0)
        part = ref[0, :, parts * cols :].astype(f32)
        out[...] = jnp.where(step == 0, part, out[...] + part)


def unpack(blocks, parts, extra=False):
    ns, rows, cols = blocks[0].shape
    cols = (cols - LANES * extra) // parts
    outs = [jax.ShapeDtypeStruct((rows, ns * len(blocks) * cols), f32)] * parts
    specs = [pl.BlockSpec((rows, len(blocks) * cols), lambda i: (0, i))] * parts
    if extra:
        outs = outs + [jax.ShapeDtypeStruct((rows, LANES), f32)]
        specs = specs + [pl.BlockSpec((rows, LANES), lambda i: (0, 0))]
    return call(
        functools.partial(unpack_kernel, len(blocks), parts),
        ns,
        tuple(blocks),
        [pl.BlockSpec((1,) + a.shape[1:], lambda i: (i, 0, 0)) for a in blocks],
        outs,
        specs,
        0,
    )


def swap_bit(block, bit, size):
    return lax.ppermute(block, "seq", [(i, i ^ bit) for i in range(size)])


def link_bits(size):
    bits = []
    bit = 2
    while bit < size:
        bits.append(bit)
        bit *= 2
    return bits


def orders(size):
    bits = link_bits(size)
    found = []
    for run in (bits, bits[::-1]):
        order = [0]
        for bit in run:
            order += [k ^ bit for k in order]
        found.append(order)
    return found


def swap_side(block):
    return lax.ppermute(block, "side", [(0, 1), (1, 0)])


def exchange(moves, waits=()):
    blocks = lax.optimization_barrier([b for b, _ in moves])
    got = [f(b) for (_, f), b in zip(moves, blocks)]
    got, values = lax.optimization_barrier((got, [box[i] for box, i in waits]))
    for (box, i), value in zip(waits, values):
        box[i] = value
    return got


def along(bit):
    return functools.partial(swap_bit, bit=bit, size=lax.axis_size("seq"))


def gather_steps(held):
    bits = link_bits(lax.axis_size("seq"))
    for pair in zip(bits, bits[::-1]):
        got = yield [(block, along(bit)) for block, bit in zip(held, pair)]
        held = [jnp.concatenate(pieces, axis=0) for pieces in zip(held, got)]
    side = jnp.concatenate(held, axis=0)
    (got,) = yield [(side, along(1))]
    return side, got


def scatter_steps(keep, away):
    bits = link_bits(lax.axis_size("seq"))
    (got,) = yield [(away, along(1))]
    length = keep.shape[0] // 2
    terms = [[t[i * length : (i + 1) * length] for t in (keep, got)] for i in range(2)]

    def total(parts, start, stop):
        return sum(t[start:stop].astype(f32) for t in parts)

    for pair in zip(bits[::-1], bits):
        sent = [total(parts, length // 2, length).astype(bf16) for parts in terms]
        got = yield [(block, along(bit)) for block, bit in zip(sent, pair)]
        length //= 2
        for parts, block in zip(terms, got):
            parts.append(block)
    return [total(parts, 0, length) for parts in terms]


def gather_one(own):
    half = own.shape[0] // 2
    return (yield from gather_steps([own[:half], own[half:]]))


def scatter_one(pair):
    blocks = yield from scatter_steps(*pair)
    return jnp.concatenate(blocks, axis=0)


def gather_two(own):
    (got,) = yield [(own, swap_side)]
    return (yield from gather_steps([own, got]))


def scatter_two(pair):
    mine, other = yield from scatter_steps(*pair)
    (got,) = yield [(other.astype(bf16), swap_side)]
    return mine + got.astype(f32)


class Ride:
    def __init__(self, steps):
        self.steps = steps
        self.result = None
        self.feed(None)

    def feed(self, got):
        try:
            self.moves = self.steps.send(got)
        except StopIteration as end:
            self.moves, self.result = None, end.value


def run(steps, riders=(), waits=(), then=(), at=None):
    main = steps if isinstance(steps, Ride) else Ride(steps)
    waits, then = list(waits), list(then)
    stage = 0
    while main.moves is not None:
        riding = riders if at is None or stage in at else ()
        active = [main] + [rider for rider in riding if rider.moves is not None]
        stage += 1
        got = exchange(
            [move for ride in active for move in ride.moves], waits.pop(0) if waits else ()
        )
        for ride in active:
            part, got = got[: len(ride.moves)], got[len(ride.moves) :]
            ride.feed(part)
        if then:
            then.pop(0)()
    return main.result


def body(
    tokens,
    positions,
    gain_attn,
    query_weight,
    key_weight,
    value_weight,
    out_weight,
    gain_ffn,
    gate_weight,
    up_weight,
    down_weight,
    cotangent,
):
    ns = lax.axis_size("seq")
    nb = lax.axis_size("pair") * lax.axis_size("side")
    batch = ("pair", "side")
    near = ("side", "seq")
    rows, width = query_weight.shape
    hidden = gate_weight.shape[1]
    head_cols = width // ns
    heads = head_cols // HD
    ffn_cols = hidden // (2 * ns * CHUNKS)
    own = tokens.shape[1]

    def swap(blocks, axes="seq"):
        return lax.all_to_all(blocks, axes, split_axis=0, concat_axis=0, tiled=True)

    def gather_z(block, axes=batch):
        return lax.all_gather(block, axes, axis=0, tiled=True)

    def scatter_z(full, axes=batch):
        return lax.psum_scatter(full, axes, scatter_dimension=0, tiled=True)

    low_gains = [gain_attn.astype(bf16), gain_ffn.astype(bf16)]
    gain_cols = jnp.pad(jnp.stack(low_gains, axis=1), ((0, 0), (0, LANES - 2)))
    w_v = gather_z(jnp.concatenate([value_weight.astype(bf16), gain_cols], axis=1))

    place = positions[0]
    marks = jnp.stack([place // 128, place % 128]).astype(bf16)
    marks = jnp.pad(marks.reshape(2, -1, LANES)[:, 0], ((0, rows - 2), (0, 0)))
    attn_blocks = pack(
        (query_weight, key_weight, out_weight.T.astype(bf16)),
        [[(m, 0, 1) for m in range(3)]],
        ns,
        marks,
    )
    attn_blocks = swap(attn_blocks)
    plans = [[(m, c, CHUNKS) for m in range(3)] for c in range(CHUNKS)]
    ffn_blocks = list(pack((gate_weight, up_weight, down_weight.T.astype(bf16)), plans, 2 * ns))
    x_own, attn_blocks = lax.optimization_barrier((tokens[0], attn_blocks))
    x_ride, dy_ride = Ride(gather_one(x_own)), Ride(gather_two(cotangent[0]))
    got = exchange(x_ride.moves + dy_ride.moves)
    x_ride.feed(got[:-1])
    dy_ride.feed(got[-1:])
    x_all = run(x_ride)
    w_v = w_v.reshape(nb, rows, -1)
    spread = jnp.broadcast_to(w_v[None, :, :, width:], (ns, nb, rows, LANES))
    w_v = w_v[:, :, :width].reshape(nb, rows, ns, head_cols).transpose(2, 0, 1, 3)
    w_v = swap(jnp.concatenate([w_v, spread], axis=3))
    w_v = w_v.transpose(1, 0, 2, 3).reshape(width, -1)
    gain_one = w_v[:, head_cols].astype(f32)
    gain_two = w_v[:, head_cols + 1].astype(f32)
    w_v = w_v[:, :head_cols]

    around = jnp.array([[[k ^ core for k in order] for order in orders(ns)] for core in range(2)])
    around = lax.axis_index("seq") ^ around.astype(jnp.int32)
    place = attn_blocks[:, :2, -LANES:].astype(f32).astype(jnp.int32)
    place = (place[:, 0] * 128 + place[:, 1]).reshape(ns, 2, own // 2)
    place = jnp.stack([jnp.take(place[:, i], around[:, i], axis=0) for i in range(2)], axis=1)
    place = place.reshape(-1)
    half_size = HD // 2
    frequency = jnp.exp(jnp.arange(half_size).astype(f32) * (-2.0 * math.log(rope_base) / HD))
    angles = place.astype(f32)[:, None] * frequency[None, :]
    cosine, sine = jnp.cos(angles), jnp.sin(angles)
    cosine = jnp.concatenate([cosine, cosine], axis=1)
    sine = jnp.concatenate([-sine, sine], axis=1)
    pos_col, pos_row = place[:, None], place[None, :]

    attn_blocks = attn_blocks.reshape(ns * rows, -1)
    w_qko = gather_z(attn_blocks[:, : 3 * head_cols])
    (w_qko, w_v, gain_one, x_all, cosine, sine, pos_col, pos_row, ffn_blocks[0]) = (
        lax.optimization_barrier(
            (w_qko, w_v, gain_one, x_all, cosine, sine, pos_col, pos_row, ffn_blocks[0])
        )
    )
    ffn_blocks[0] = swap(ffn_blocks[0], near).reshape(2 * ns * rows, -1)

    constants = (cosine, sine, pos_col, pos_row)
    normed, queries, keys, values, attended, kept, away = front(
        x_all, gain_one[None], w_qko, w_v, *constants, width // HD
    )
    w_ffn = [gather_z(ffn_blocks[0], "pair")]

    def second():
        ffn_blocks[1] = swap(ffn_blocks[1], near).reshape(2 * ns * rows, -1)

    attn_own = run(
        scatter_one((kept, away)),
        [dy_ride],
        [[(ffn_blocks, 1)], [(w_ffn, 0), (ffn_blocks, 1)]],
        [second],
    )
    w_ffn.append(gather_z(ffn_blocks[1][:, : 2 * ffn_cols], "pair"))
    w_ffn.append(gather_z(ffn_blocks[1][:, 2 * ffn_cols :], "pair"))
    attn_mass = attn_own[:, width]
    x_own_f = x_own.astype(f32)
    hidden_own = x_own_f + attn_own[:, :width]
    scale_two = norm_scale(hidden_own)
    unit_two = hidden_own * scale_two
    normed_ffn = run(
        gather_two((unit_two * gain_two).astype(bf16)),
        [dy_ride],
        [[], [(w_ffn, 1)]],
    )
    dy_all = dy_ride.result

    acts, backs, sums, gain_sums = [], [], [], []
    chunks = [Chunk(w_ffn[0], w_ffn[0], 2)]
    for c in range(CHUNKS):
        act, grads = ffn(normed_ffn, dy_all, chunks[c])
        acts.append(act)
        backs.append(grads)
        if c + 1 == CHUNKS:
            break
        part, gains = ffn_sums(normed_ffn, dy_all, act, grads, chunks[c])
        gain_sums.append(gains)
        acts[c], backs[c], part, w_ffn[1:] = lax.optimization_barrier(
            (act, grads, part, w_ffn[1:])
        )
        chunks.append(Chunk(w_ffn[1], w_ffn[2], 0))
        sums.append(scatter_z(part, "pair"))
    grads_pair = back(backs, chunks, 0)

    def home(part, axes="seq"):
        return swap(part.reshape(lax.axis_size(axes), rows, -1), axes)

    made = []

    def last_sums():
        part, gains = ffn_sums(normed_ffn, dy_all, acts[-1], backs[-1], chunks[-1])
        gain_sums.append(gains)
        made.append(part)

    def leave():
        sums.append(scatter_z(made[0], "pair"))

    def output():
        made.append(back(acts, chunks, 1))

    grad_normed_two = run(
        scatter_two(grads_pair),
        (),
        [[(acts, 1), (backs, 1)], [(made, 0)], [(sums, 0), (acts, 0)], [(made, 1)]],
        [last_sums, leave, output],
    )
    grad_hidden = cotangent[0].astype(f32) + norm_back(
        grad_normed_two, unit_two, scale_two, gain_two
    )

    ffn_sum = [home(sums[0], near)]
    out_ride = Ride(scatter_two(made[1]))
    waits = [[], [(ffn_sum, 0), (sums, 1)]]
    left = len(link_bits(ns))
    branch = run(gather_one(grad_hidden.astype(bf16)), [out_ride], waits, (), (left,))
    out_sum = branch_sums(branch, attended)
    moves = out_ride.moves
    branch, out_sum, sent = lax.optimization_barrier((branch, out_sum, [b for b, _ in moves]))
    flying = [f(b) for (_, f), b in zip(moves, sent)]
    out_sum = scatter_z(out_sum)
    dq, dk, dv, qkv_local = rear(
        branch, queries, keys, values, constants, normed, w_qko, w_v, gain_sums
    )
    ffn_sum.append(home(sums[1], near))
    dq, dk, dv, qkv_local, ffn_sum, flying, out_sum = lax.optimization_barrier(
        (dq, dk, dv, qkv_local, ffn_sum, flying, out_sum)
    )
    out_ride.feed(flying)
    qkv_sum = scatter_z(qkv_local)
    part = enter_back([dq, dk, dv], w_qko, w_v)
    grad_normed = run(scatter_one(part), [out_ride], at=range(left - 1))
    moves = out_ride.moves
    qkv_sum, sent = lax.optimization_barrier((qkv_sum, [b for b, _ in moves]))
    out_ride.feed([f(b) for (_, f), b in zip(moves, sent)])
    layer_out = (hidden_own + out_ride.result).astype(bf16)
    scale_one = norm_scale(x_own_f)
    input_grad = (
        grad_hidden + norm_back(grad_normed, x_own_f * scale_one, scale_one, gain_one)
    ).astype(bf16)

    gate_grad, up_grad, down_grad = unpack(ffn_sum, 3)
    attn_sums = home(jnp.concatenate([out_sum, qkv_sum], axis=1))
    out_grad, query_grad, key_grad, value_grad, gains = unpack([attn_sums], 4, True)
    out_grad, down_grad = out_grad.T, down_grad.T
    return (
        layer_out[None],
        input_grad[None],
        attn_mass[None],
        gains[:, 0] / low_gains[0].astype(f32),
        query_grad,
        key_grad,
        value_grad,
        out_grad,
        gains[:, 1] / low_gains[1].astype(f32),
        gate_grad,
        up_grad,
        down_grad,
    )


def solution(mesh):
    nb, ns = mesh.shape["batch"], mesh.shape["seq"]
    mesh = jax.sharding.Mesh(mesh.devices.reshape(nb // 2, 2, ns), ("pair", "side", "seq"))
    batch = ("pair", "side")
    both = ("pair", "side", "seq")
    token_spec = P(batch, "seq", None)
    row_spec = P(both, None)
    col_spec = P(None, both)
    return jax.shard_map(
        body,
        mesh=mesh,
        in_specs=(
            token_spec,
            P(batch, "seq"),
            P(both),
            row_spec,
            row_spec,
            row_spec,
            col_spec,
            P(both),
            row_spec,
            row_spec,
            col_spec,
            token_spec,
        ),
        out_specs=(
            token_spec,
            token_spec,
            P(batch, "seq"),
            P(both),
            row_spec,
            row_spec,
            row_spec,
            col_spec,
            P(both),
            row_spec,
            row_spec,
            col_spec,
        ),
        check_vma=False,
    )
```

```python
import functools
import math

import jax
import jax.numpy as jnp
from jax import lax
from jax.experimental import pallas as pl
from jax.experimental.pallas import tpu as pltpu
from jax.sharding import PartitionSpec as P

HD = 128
LANES = 128
epsilon = 1e-05
rope_base = 10000.0
score_bias = -math.log(4096.0)
score_scale = 1.0 / math.sqrt(HD)
f32 = jnp.float32
bf16 = jnp.bfloat16
CHUNKS = 2
TILE = 256
MIB = 1 << 20


def dot(left, right):
    return jnp.dot(left, right, preferred_element_type=f32)


def dot_t(left, right):
    return lax.dot_general(left, right, (((1,), (1,)), ((), ())), preferred_element_type=f32)


def t_dot(left, right):
    return lax.dot_general(left, right, (((0,), (0,)), ((), ())), preferred_element_type=f32)


def norm_scale(values):
    return lax.rsqrt(jnp.mean(values * values, axis=-1, keepdims=True) + epsilon)


def norm_back(grad_normed, unit_rows, scale_rows, gain_vec):
    grad_unit = grad_normed * gain_vec
    return scale_rows * (
        grad_unit - unit_rows * jnp.mean(grad_unit * unit_rows, axis=-1, keepdims=True)
    )


def columns(array, at, cols):
    return pl.BlockSpec((array.shape[0], cols), lambda *_: (0, at), pipeline_mode=pl.Buffered(1))


def whole(shape):
    zeros = (0,) * len(shape)
    return pl.BlockSpec(shape, lambda *_: zeros, pipeline_mode=pl.Buffered(1))


def rows_of(tile, cols):
    return pl.BlockSpec((tile, cols), lambda i, *_: (i, 0))


def call(kernel, steps, ins, in_specs, outs, out_specs, flops, vmem=60, scalars=0):
    size = sum(math.prod(a.shape) * a.dtype.itemsize for a in (*ins, *outs))
    result = pl.pallas_call(
        kernel,
        grid_spec=pltpu.PrefetchScalarGridSpec(
            num_scalar_prefetch=scalars,
            grid=(steps,),
            in_specs=in_specs,
            out_specs=out_specs,
        ),
        out_shape=outs,
        compiler_params=pltpu.CompilerParams(
            dimension_semantics=("arbitrary",), vmem_limit_bytes=vmem * MIB
        ),
        cost_estimate=pl.CostEstimate(flops=flops, bytes_accessed=size, transcendentals=0),
    )(*ins)
    return result[0] if len(outs) == 1 else result


def pack_kernel(plans, *refs):
    ins, outs = refs[: -len(plans)], refs[-len(plans) :]
    for plan, out_ref in zip(plans, outs):
        at = 0
        for m, part, parts in plan:
            cols = ins[m].shape[1] // parts
            value = ins[m][:, part * cols : (part + 1) * cols]
            out_ref[0, :, at : at + cols] = value.astype(bf16)
            at += cols


def pack(arrays, plans, ns, marks=None):
    rows = arrays[0].shape[0]
    specs = [pl.BlockSpec((rows, a.shape[1] // ns), lambda i: (0, i)) for a in arrays]
    widths = [a.shape[1] // ns for a in arrays]
    if marks is not None:
        plans = [plan + [(len(arrays), 0, 1)] for plan in plans]
        arrays = arrays + (marks,)
        specs.append(whole(marks.shape))
        widths.append(marks.shape[1])
    cols = [sum(widths[m] // parts for m, _, parts in plan) for plan in plans]
    return call(
        functools.partial(pack_kernel, plans),
        ns,
        arrays,
        specs,
        [jax.ShapeDtypeStruct((ns, rows, n), bf16) for n in cols],
        [pl.BlockSpec((1, rows, n), lambda i: (i, 0, 0)) for n in cols],
        0,
    )


def turn(values, cosine, sine):
    return values * cosine + pltpu.roll(values, HD // 2, 1) * sine


def halves(length, cols):
    tile = min(TILE, length // 2)
    count = length // 2 // tile
    shape = jax.ShapeDtypeStruct((length // 2, cols), bf16)
    return tile, 2 * count, [shape] * 2, pair_specs(length, cols, tile)


def pair_specs(length, cols, tile):
    count = length // 2 // tile
    return [
        pl.BlockSpec((tile, cols), lambda i, *_: (jnp.minimum(i, count - 1), 0)),
        pl.BlockSpec((tile, cols), lambda i, *_: (jnp.maximum(i - count, 0), 0)),
    ]


def either(pair):
    first = pl.program_id(0) < pl.num_programs(0) // 2
    return jnp.where(first, pair[0][...], pair[1][...])


def store_half(value, outs):
    first = pl.program_id(0) < pl.num_programs(0) // 2

    @pl.when(first)
    def _():
        outs[0][...] = value

    @pl.when(jnp.logical_not(first))
    def _():
        outs[1][...] = value


def later(i, first, count):
    return jnp.clip(i - first, 0, count - 1)


def front_kernel(
    heads_all, steps, xa, xb, gain_ref, wq, wk, wv, wo, cos, sin, col, row, *refs
):
    n_ref, qo, ko, vo, oo, keep, away, qkv, mass = refs
    i = pl.program_id(0)
    tile = n_ref.shape[0]
    cols = wq.shape[1]

    @pl.when(i < steps)
    def _():
        rows = jnp.where(i < steps // 2, xa[...], xb[...]).astype(f32)
        normed = (rows * norm_scale(rows) * gain_ref[...]).astype(bf16)
        n_ref[...] = normed
        at = pl.ds(pl.multiple_of(i * tile, tile), tile)
        for j, w in enumerate((wq, wk, wv)):
            qkv[at, j * cols : (j + 1) * cols] = dot(normed, w[...])

    @pl.when(i == steps - 1)
    def _():
        cosine, sine = cos[...], sin[...]
        for h in range(cols // HD):
            head = slice(h * HD, (h + 1) * HD)
            queries = turn(qkv[:, h * HD : (h + 1) * HD], cosine, sine).astype(bf16)
            keys = turn(qkv[:, cols + h * HD : cols + (h + 1) * HD], cosine, sine).astype(bf16)
            values = qkv[:, 2 * cols + h * HD : 2 * cols + (h + 1) * HD].astype(bf16)
            qo[:, head] = queries
            ko[:, head] = keys
            vo[:, head] = values
            for j in range(steps):
                at = slice(j * tile, (j + 1) * tile)
                scores = dot_t(queries[at], keys) * score_scale + score_bias
                weights = jnp.where(row[...] <= col[at, :], jax.nn.sigmoid(scores), 0.0)
                oo[at, head] = dot(weights.astype(bf16), values).astype(bf16)
                part = jnp.sum(weights, axis=1, keepdims=True) * (1.0 / heads_all)
                part = jnp.broadcast_to(part, (tile, LANES))
                mass[at, :] = part if h == 0 else mass[at, :] + part

    def projected():
        at = pl.ds(pl.multiple_of((i - steps) * tile, tile), tile)
        value = dot_t(oo[at, :], wo[...]).astype(bf16)
        return jnp.concatenate([value, mass[at, :].astype(bf16)], axis=1)

    @pl.when((i >= steps) & (i < steps + steps // 2))
    def _():
        keep[...] = projected()

    @pl.when(i >= steps + steps // 2)
    def _():
        away[...] = projected()


def front(x_pair, gain, w_qko, w_v, cosine, sine, pos_col, pos_row, heads_all):
    length, width = 2 * x_pair[0].shape[0], x_pair[0].shape[1]
    cols = w_v.shape[1]
    tile = min(TILE, length // 2)
    steps = length // tile
    half = steps // 2
    constants = (cosine, sine, pos_col, pos_row)
    rows = jax.ShapeDtypeStruct((length, cols), bf16)
    sides = jax.ShapeDtypeStruct((length // 2, width + LANES), bf16)
    return pl.pallas_call(
        functools.partial(front_kernel, heads_all, steps),
        grid=(2 * steps,),
        in_specs=[
            pl.BlockSpec((tile, width), lambda i: (later(i, 0, half), 0)),
            pl.BlockSpec((tile, width), lambda i: (later(i, half, half), 0)),
            whole(gain.shape),
            columns(w_qko, 0, cols),
            columns(w_qko, 1, cols),
            whole(w_v.shape),
            columns(w_qko, 2, cols),
        ]
        + [whole(a.shape) for a in constants],
        out_specs=[pl.BlockSpec((tile, width), lambda i: (later(i, 0, steps), 0))]
        + [pl.BlockSpec((length, cols), lambda i: (0, 0))] * 4
        + [
            pl.BlockSpec((tile, width + LANES), lambda i: (later(i, steps, half), 0)),
            pl.BlockSpec((tile, width + LANES), lambda i: (later(i, steps + half, half), 0)),
        ],
        out_shape=[jax.ShapeDtypeStruct((length, width), bf16)] + [rows] * 4 + [sides] * 2,
        scratch_shapes=[pltpu.VMEM((length, 3 * cols), f32), pltpu.VMEM((length, LANES), f32)],
        compiler_params=pltpu.CompilerParams(
            dimension_semantics=("arbitrary",), vmem_limit_bytes=60 * MIB
        ),
        cost_estimate=pl.CostEstimate(
            flops=8 * length * width * cols,
            bytes_accessed=12 * length * width,
            transcendentals=0,
        ),
    )(*x_pair, gain, w_qko, w_qko, w_v, w_qko, *constants)


def ffn_kernel(na_ref, nb_ref, da_ref, db_ref, gu_ref, down_ref, act_ref, back_ref):
    cols = act_ref.shape[1]
    gated = dot(either((na_ref, nb_ref)), gu_ref[...])
    grad_act = dot(either((da_ref, db_ref)), down_ref[...])
    gate, up = gated[:, :cols], gated[:, cols:]
    sig = jax.nn.sigmoid(gate)
    silu = gate * sig
    act_ref[...] = (silu * up).astype(bf16)
    back_ref[:, :cols] = (grad_act * up * sig * (1.0 + gate * (1.0 - sig))).astype(bf16)
    back_ref[:, cols:] = (grad_act * silu).astype(bf16)


def ffn(n_pair, d_pair, w):
    length, width = 2 * n_pair[0].shape[0], n_pair[0].shape[1]
    cols = w.cols
    tile = min(2 * TILE, length // 2)
    return call(
        ffn_kernel,
        length // tile,
        (*n_pair, *d_pair, w.gated, w.down),
        pair_specs(length, width, tile) * 2 + w.specs(),
        [
            jax.ShapeDtypeStruct((length, cols), bf16),
            jax.ShapeDtypeStruct((length, 2 * cols), bf16),
        ],
        [rows_of(tile, cols), rows_of(tile, 2 * cols)],
        6 * length * width * cols,
    )


def cols_of(length, tile):
    return pl.BlockSpec((length, tile), lambda i, *_: (0, i))


def t_dot_pair(pair, right):
    half = pair[0].shape[0]
    return t_dot(pair[0][...], right[:half, :]) + t_dot(pair[1][...], right[half:, :])


def ffn_sums_kernel(na_ref, nb_ref, da_ref, db_ref, act_ref, back_ref, gu_ref, sum_ref, gain_ref):
    cols = act_ref.shape[1]
    gated = t_dot_pair((na_ref, nb_ref), back_ref)
    sum_ref[:, : 2 * cols] = gated.astype(bf16)
    sum_ref[:, 2 * cols :] = t_dot_pair((da_ref, db_ref), act_ref).astype(bf16)
    gain = jnp.sum(gated * gu_ref[...].astype(f32), axis=1, keepdims=True)
    gain_ref[...] = jnp.broadcast_to(gain, gain_ref.shape)


def ffn_sums(n_pair, d_pair, act, back, w):
    half, width = n_pair[0].shape
    cols = act.shape[1]
    tile = min(2 * TILE, width)
    return call(
        ffn_sums_kernel,
        width // tile,
        (*n_pair, *d_pair, act, back, w.gated),
        [cols_of(half, tile)] * 4
        + [whole(act.shape), whole(back.shape), rows_of(tile, 2 * cols)],
        [
            jax.ShapeDtypeStruct((width, 3 * cols), bf16),
            jax.ShapeDtypeStruct((width, LANES), f32),
        ],
        [rows_of(tile, 3 * cols), rows_of(tile, LANES)],
        12 * half * width * cols,
    )


def branch_sums_kernel(a_ref, b_ref, o_ref, sum_ref):
    sum_ref[...] = t_dot_pair((a_ref, b_ref), o_ref).astype(bf16)


def branch_sums(pair, attended):
    half, width = pair[0].shape
    cols = attended.shape[1]
    tile = min(2 * TILE, width)
    return call(
        branch_sums_kernel,
        width // tile,
        (*pair, attended),
        [cols_of(half, tile)] * 2 + [whole(attended.shape)],
        [jax.ShapeDtypeStruct((width, cols), bf16)],
        [rows_of(tile, cols)],
        4 * half * width * cols,
    )


def back_kernel(count, *refs):
    lefts, rights, outs = refs[:count], refs[count : 2 * count], refs[2 * count :]
    total = sum(dot_t(left[...], right[...]) for left, right in zip(lefts, rights))
    store_half(total.astype(bf16), outs)


def enter_back(lefts, w_qko, w_v):
    length, cols = lefts[0].shape
    width = w_v.shape[0]
    tile, steps, outs, specs = halves(length, width)
    return call(
        functools.partial(back_kernel, 3),
        steps,
        (*lefts, w_qko, w_qko, w_v),
        [rows_of(tile, cols)] * 3
        + [columns(w_qko, 0, cols), columns(w_qko, 1, cols), whole(w_v.shape)],
        outs,
        specs,
        6 * length * width * cols,
    )


class Chunk:
    def __init__(self, gated, down, at):
        self.gated, self.down, self.at = gated, down, at
        self.cols = down.shape[1] // (at + 1)

    def specs(self):
        return [columns(self.gated, 0, 2 * self.cols), columns(self.down, self.at, self.cols)]


def back(lefts, chunks, which):
    length = lefts[0].shape[0]
    width = chunks[0].gated.shape[0]
    tile, steps, outs, specs = halves(length, width)
    return call(
        functools.partial(back_kernel, len(lefts)),
        steps,
        (*lefts, *((w.gated, w.down)[which] for w in chunks)),
        [rows_of(tile, a.shape[1]) for a in lefts] + [w.specs()[which] for w in chunks],
        outs,
        specs,
        2 * length * width * sum(a.shape[1] for a in lefts),
    )


def rear_kernel(
    steps, ba, bb, wo, q_ref, k_ref, v_ref, cos, sin, col, row, n_ref, wq, wk, wv, g0, g1, *refs
):
    dq, dk, dv, out_ref, gain_ref, grads = refs
    i = pl.program_id(0)
    tile = ba.shape[0]
    cols = wo.shape[1]

    @pl.when(i < steps)
    def _():
        at = pl.ds(pl.multiple_of(i * tile, tile), tile)
        rows = jnp.where(i < steps // 2, ba[...], bb[...])
        grads[at, :] = dot(rows, wo[...]).astype(bf16)

    @pl.when(i == steps - 1)
    def _():
        cosine, sine = cos[...], -sin[...]
        for h in range(cols // HD):
            head = slice(h * HD, (h + 1) * HD)
            queries, keys, values = q_ref[:, head], k_ref[:, head], v_ref[:, head]
            gradient = grads[:, head]
            grad_keys = grad_values = 0.0
            for j in range(steps):
                at = slice(j * tile, (j + 1) * tile)
                scores = dot_t(keys, queries[at]) * score_scale + score_bias
                weights = jnp.where(col[...] <= row[:, at], jax.nn.sigmoid(scores), 0.0)
                grad_weights = dot_t(values, gradient[at])
                grad_scores = (grad_weights * weights * (1.0 - weights)).astype(bf16)
                grad_values = grad_values + dot(weights.astype(bf16), gradient[at])
                grad_keys = grad_keys + dot(grad_scores, queries[at])
                grad_query = t_dot(grad_scores, keys) * score_scale
                dq[at, head] = turn(grad_query, cosine[at], sine[at]).astype(bf16)
            dk[:, head] = turn(grad_keys * score_scale, cosine, sine).astype(bf16)
            dv[:, head] = grad_values.astype(bf16)

    @pl.when(i >= steps)
    def _():
        gain = 0.0
        for j, (ref, w) in enumerate(((dq, wq), (dk, wk), (dv, wv))):
            part = t_dot(n_ref[...], ref[...])
            out_ref[:, j * cols : (j + 1) * cols] = part.astype(bf16)
            gain = gain + jnp.sum(part * w[...].astype(f32), axis=1, keepdims=True)
        lane = lax.broadcasted_iota(jnp.int32, g0.shape, 1)
        gain_ref[...] = jnp.where(lane == 0, gain, g0[...] + g1[...])


def rear(pair, queries, keys, values, constants, normed, w_qko, w_v, gain_sums):
    length, width = normed.shape
    cols = w_v.shape[1]
    tile = min(TILE, length // 2)
    steps = length // tile
    half = steps // 2
    block = min(2 * TILE, width)
    blocks = width // block
    rows = jax.ShapeDtypeStruct((length, cols), bf16)
    place = lambda at: pl.BlockSpec((block, cols), lambda i: (later(i, steps, blocks), at))
    return pl.pallas_call(
        functools.partial(rear_kernel, steps),
        grid=(steps + blocks,),
        in_specs=[
            pl.BlockSpec((tile, width), lambda i: (later(i, 0, half), 0)),
            pl.BlockSpec((tile, width), lambda i: (later(i, half, half), 0)),
            columns(w_qko, 2, cols),
        ]
        + [whole(a.shape) for a in (queries, keys, values, *constants)]
        + [pl.BlockSpec((length, block), lambda i: (0, later(i, steps, blocks)))]
        + [place(0), place(1), place(0)]
        + [pl.BlockSpec((block, LANES), lambda i: (later(i, steps, blocks), 0))] * 2,
        out_specs=[pl.BlockSpec((length, cols), lambda i: (0, 0))] * 3
        + [pl.BlockSpec((block, n), lambda i: (later(i, steps, blocks), 0)) for n in (3 * cols, LANES)],
        out_shape=[rows] * 3
        + [
            jax.ShapeDtypeStruct((width, 3 * cols), bf16),
            jax.ShapeDtypeStruct((width, LANES), f32),
        ],
        scratch_shapes=[pltpu.VMEM((length, cols), bf16)],
        compiler_params=pltpu.CompilerParams(
            dimension_semantics=("arbitrary",), vmem_limit_bytes=60 * MIB
        ),
        cost_estimate=pl.CostEstimate(
            flops=8 * length * width * cols,
            bytes_accessed=8 * length * width,
            transcendentals=0,
        ),
    )(*pair, w_qko, queries, keys, values, *constants, normed, w_qko, w_qko, w_v, *gain_sums)


def unpack_kernel(count, parts, *refs):
    ins, outs = refs[:count], refs[count:]
    cols = outs[0].shape[1] // count
    for c, ref in enumerate(ins):
        for i in range(parts):
            outs[i][:, c * cols : (c + 1) * cols] = ref[0, :, i * cols : (i + 1) * cols].astype(f32)
    for i, out in enumerate(outs[parts:]):
        step = pl.program_id(0)
        part = ref[0, :, parts * cols :].astype(f32)
        out[...] = jnp.where(step == 0, part, out[...] + part)


def unpack(blocks, parts, extra=False):
    ns, rows, cols = blocks[0].shape
    cols = (cols - LANES * extra) // parts
    outs = [jax.ShapeDtypeStruct((rows, ns * len(blocks) * cols), f32)] * parts
    specs = [pl.BlockSpec((rows, len(blocks) * cols), lambda i: (0, i))] * parts
    if extra:
        outs = outs + [jax.ShapeDtypeStruct((rows, LANES), f32)]
        specs = specs + [pl.BlockSpec((rows, LANES), lambda i: (0, 0))]
    return call(
        functools.partial(unpack_kernel, len(blocks), parts),
        ns,
        tuple(blocks),
        [pl.BlockSpec((1,) + a.shape[1:], lambda i: (i, 0, 0)) for a in blocks],
        outs,
        specs,
        0,
    )


def swap_bit(block, bit, size):
    return lax.ppermute(block, "seq", [(i, i ^ bit) for i in range(size)])


def link_bits(size):
    bits = []
    bit = 2
    while bit < size:
        bits.append(bit)
        bit *= 2
    return bits


def orders(size):
    bits = link_bits(size)
    found = []
    for run in (bits, bits[::-1]):
        order = [0]
        for bit in run:
            order += [k ^ bit for k in order]
        found.append(order)
    return found


def swap_side(block):
    return lax.ppermute(block, "side", [(0, 1), (1, 0)])


def exchange(moves, waits=()):
    blocks = lax.optimization_barrier([b for b, _ in moves])
    got = [f(b) for (_, f), b in zip(moves, blocks)]
    got, values = lax.optimization_barrier((got, [box[i] for box, i in waits]))
    for (box, i), value in zip(waits, values):
        box[i] = value
    return got


def along(bit):
    return functools.partial(swap_bit, bit=bit, size=lax.axis_size("seq"))


def gather_steps(held):
    bits = link_bits(lax.axis_size("seq"))
    for pair in zip(bits, bits[::-1]):
        got = yield [(block, along(bit)) for block, bit in zip(held, pair)]
        held = [jnp.concatenate(pieces, axis=0) for pieces in zip(held, got)]
    side = jnp.concatenate(held, axis=0)
    (got,) = yield [(side, along(1))]
    return side, got


def scatter_steps(keep, away):
    bits = link_bits(lax.axis_size("seq"))
    (got,) = yield [(away, along(1))]
    length = keep.shape[0] // 2
    terms = [[t[i * length : (i + 1) * length] for t in (keep, got)] for i in range(2)]

    def total(parts, start, stop):
        return sum(t[start:stop].astype(f32) for t in parts)

    for pair in zip(bits[::-1], bits):
        sent = [total(parts, length // 2, length).astype(bf16) for parts in terms]
        got = yield [(block, along(bit)) for block, bit in zip(sent, pair)]
        length //= 2
        for parts, block in zip(terms, got):
            parts.append(block)
    return [total(parts, 0, length) for parts in terms]


def gather_one(own):
    half = own.shape[0] // 2
    return (yield from gather_steps([own[:half], own[half:]]))


def scatter_one(pair):
    blocks = yield from scatter_steps(*pair)
    return jnp.concatenate(blocks, axis=0)


def gather_two(own):
    (got,) = yield [(own, swap_side)]
    return (yield from gather_steps([own, got]))


def scatter_two(pair):
    mine, other = yield from scatter_steps(*pair)
    (got,) = yield [(other.astype(bf16), swap_side)]
    return mine + got.astype(f32)


def sum_all(block):
    bit = 1
    while bit < lax.axis_size("seq"):
        (got,) = yield [(block, along(bit))]
        block = block + got
        bit *= 2
    (got,) = yield [(block, swap_side)]
    block = block + got
    bit = 1
    while bit < lax.axis_size("pair"):
        (got,) = yield [(block, swap_pair(bit))]
        block = block + got
        bit *= 2
    return block


def swap_pair(bit):
    pairs = [(i, i ^ bit) for i in range(lax.axis_size("pair"))]
    return lambda block: lax.ppermute(block, "pair", pairs)


class Ride:
    def __init__(self, steps):
        self.steps = steps
        self.result = None
        self.feed(None)

    def feed(self, got):
        try:
            self.moves = self.steps.send(got)
        except StopIteration as end:
            self.moves, self.result = None, end.value


def run(steps, riders=(), waits=(), then=(), at=None):
    main = steps if isinstance(steps, Ride) else Ride(steps)
    waits, then = list(waits), list(then)
    stage = 0
    while main.moves is not None:
        riding = [r for r in riders if at is None or stage in at.get(r, range(8))]
        active = [main] + [rider for rider in riding if rider.moves is not None]
        stage += 1
        got = exchange(
            [move for ride in active for move in ride.moves], waits.pop(0) if waits else ()
        )
        for ride in active:
            part, got = got[: len(ride.moves)], got[len(ride.moves) :]
            ride.feed(part)
        if then:
            then.pop(0)()
    return main.result


def body(
    tokens,
    positions,
    gain_attn,
    query_weight,
    key_weight,
    value_weight,
    out_weight,
    gain_ffn,
    gate_weight,
    up_weight,
    down_weight,
    cotangent,
):
    ns = lax.axis_size("seq")
    nb = lax.axis_size("pair") * lax.axis_size("side")
    batch = ("pair", "side")
    near = ("side", "seq")
    rows, width = query_weight.shape
    hidden = gate_weight.shape[1]
    head_cols = width // ns
    heads = head_cols // HD
    ffn_cols = hidden // (2 * ns * CHUNKS)
    own = tokens.shape[1]

    def swap(blocks, axes="seq"):
        return lax.all_to_all(blocks, axes, split_axis=0, concat_axis=0, tiled=True)

    def gather_z(block, axes=batch):
        return lax.all_gather(block, axes, axis=0, tiled=True)

    def scatter_z(full, axes=batch):
        return lax.psum_scatter(full, axes, scatter_dimension=0, tiled=True)

    low_gains = [gain_attn.astype(bf16), gain_ffn.astype(bf16)]
    gain_cols = jnp.pad(jnp.stack(low_gains, axis=1), ((0, 0), (0, LANES - 2)))
    w_v = gather_z(jnp.concatenate([value_weight.astype(bf16), gain_cols], axis=1))

    place = positions[0]
    marks = jnp.stack([place // 128, place % 128]).astype(bf16)
    marks = jnp.pad(marks.reshape(2, -1, LANES)[:, 0], ((0, rows - 2), (0, 0)))
    attn_blocks = pack(
        (query_weight, key_weight, out_weight.T.astype(bf16)),
        [[(m, 0, 1) for m in range(3)]],
        ns,
        marks,
    )
    attn_blocks = swap(attn_blocks)
    plans = [[(m, c, CHUNKS) for m in range(3)] for c in range(CHUNKS)]
    ffn_blocks = list(pack((gate_weight, up_weight, down_weight.T.astype(bf16)), plans, 2 * ns))
    x_own, attn_blocks = lax.optimization_barrier((tokens[0], attn_blocks))
    x_ride, dy_ride = Ride(gather_one(x_own)), Ride(gather_two(cotangent[0]))
    got = exchange(x_ride.moves + dy_ride.moves)
    x_ride.feed(got[:-1])
    dy_ride.feed(got[-1:])
    x_all = run(x_ride)
    w_v = w_v.reshape(nb, rows, -1)
    spread = jnp.broadcast_to(w_v[None, :, :, width:], (ns, nb, rows, LANES))
    w_v = w_v[:, :, :width].reshape(nb, rows, ns, head_cols).transpose(2, 0, 1, 3)
    w_v = swap(jnp.concatenate([w_v, spread], axis=3))
    w_v = w_v.transpose(1, 0, 2, 3).reshape(width, -1)
    gain_one = w_v[:, head_cols].astype(f32)
    gain_two = w_v[:, head_cols + 1].astype(f32)
    w_v = w_v[:, :head_cols]

    around = jnp.array([[[k ^ core for k in order] for order in orders(ns)] for core in range(2)])
    around = lax.axis_index("seq") ^ around.astype(jnp.int32)
    place = attn_blocks[:, :2, -LANES:].astype(f32).astype(jnp.int32)
    place = (place[:, 0] * 128 + place[:, 1]).reshape(ns, 2, own // 2)
    place = jnp.stack([jnp.take(place[:, i], around[:, i], axis=0) for i in range(2)], axis=1)
    place = place.reshape(-1)
    half_size = HD // 2
    frequency = jnp.exp(jnp.arange(half_size).astype(f32) * (-2.0 * math.log(rope_base) / HD))
    angles = place.astype(f32)[:, None] * frequency[None, :]
    cosine, sine = jnp.cos(angles), jnp.sin(angles)
    cosine = jnp.concatenate([cosine, cosine], axis=1)
    sine = jnp.concatenate([-sine, sine], axis=1)
    pos_col, pos_row = place[:, None], place[None, :]

    attn_blocks = attn_blocks.reshape(ns * rows, -1)
    w_qko = gather_z(attn_blocks[:, : 3 * head_cols])
    (w_qko, w_v, gain_one, x_all, cosine, sine, pos_col, pos_row, ffn_blocks[0]) = (
        lax.optimization_barrier(
            (w_qko, w_v, gain_one, x_all, cosine, sine, pos_col, pos_row, ffn_blocks[0])
        )
    )
    ffn_blocks[0] = swap(ffn_blocks[0], near).reshape(2 * ns * rows, -1)

    constants = (cosine, sine, pos_col, pos_row)
    normed, queries, keys, values, attended, kept, away = front(
        x_all, gain_one[None], w_qko, w_v, *constants, width // HD
    )
    w_ffn = [gather_z(ffn_blocks[0], "pair")]

    def second():
        ffn_blocks[1] = swap(ffn_blocks[1], near).reshape(2 * ns * rows, -1)

    attn_own = run(
        scatter_one((kept, away)),
        [dy_ride],
        [[(ffn_blocks, 1)], [(w_ffn, 0), (ffn_blocks, 1)]],
        [second],
    )
    w_ffn.append(gather_z(ffn_blocks[1][:, : 2 * ffn_cols], "pair"))
    w_ffn.append(gather_z(ffn_blocks[1][:, 2 * ffn_cols :], "pair"))
    attn_mass = attn_own[:, width]
    x_own_f = x_own.astype(f32)
    hidden_own = x_own_f + attn_own[:, :width]
    scale_two = norm_scale(hidden_own)
    unit_two = hidden_own * scale_two
    normed_ffn = run(
        gather_two((unit_two * gain_two).astype(bf16)),
        [dy_ride],
        [[], [(w_ffn, 1)]],
    )
    dy_all = dy_ride.result

    acts, backs, sums, gain_sums = [], [], [], []
    chunks = [Chunk(w_ffn[0], w_ffn[0], 2)]
    for c in range(CHUNKS):
        act, grads = ffn(normed_ffn, dy_all, chunks[c])
        acts.append(act)
        backs.append(grads)
        if c + 1 == CHUNKS:
            break
        part, gains = ffn_sums(normed_ffn, dy_all, act, grads, chunks[c])
        gain_sums.append(gains)
        acts[c], backs[c], part, w_ffn[1:] = lax.optimization_barrier(
            (act, grads, part, w_ffn[1:])
        )
        chunks.append(Chunk(w_ffn[1], w_ffn[2], 0))
        sums.append(scatter_z(part, "pair"))
    grads_pair = back(backs, chunks, 0)

    def home(part, axes="seq"):
        return swap(part.reshape(lax.axis_size(axes), rows, -1), axes)

    made = []

    def last_sums():
        part, gains = ffn_sums(normed_ffn, dy_all, acts[-1], backs[-1], chunks[-1])
        gain_sums.append(gains)
        made.append(part)

    def leave():
        sums.append(scatter_z(made[0], "pair"))

    def output():
        made.append(back(acts, chunks, 1))

    grad_normed_two = run(
        scatter_two(grads_pair),
        (),
        [[(acts, 1), (backs, 1)], [(made, 0)], [(sums, 0), (acts, 0)], [(made, 1)]],
        [last_sums, leave, output],
    )
    grad_hidden = cotangent[0].astype(f32) + norm_back(
        grad_normed_two, unit_two, scale_two, gain_two
    )

    ffn_sum = [home(sums[0], near)]
    out_ride = Ride(scatter_two(made[1]))
    waits = [[], [(ffn_sum, 0), (sums, 1)]]
    left = len(link_bits(ns))
    branch = run(gather_one(grad_hidden.astype(bf16)), [out_ride], waits, (), {out_ride: (left,)})
    out_sum = branch_sums(branch, attended)
    moves = out_ride.moves
    branch, out_sum, sent = lax.optimization_barrier((branch, out_sum, [b for b, _ in moves]))
    flying = [f(b) for (_, f), b in zip(moves, sent)]
    out_sum = scatter_z(out_sum)
    dq, dk, dv, qkv_local, gains = rear(
        branch, queries, keys, values, constants, normed, w_qko, w_v, gain_sums
    )
    ffn_sum.append(home(sums[1], near))
    dq, dk, dv, qkv_local, ffn_sum, flying, out_sum = lax.optimization_barrier(
        (dq, dk, dv, qkv_local, ffn_sum, flying, out_sum)
    )
    out_ride.feed(flying)
    qkv_sum = scatter_z(qkv_local)
    part = enter_back([dq, dk, dv], w_qko, w_v)
    gains = jnp.stack([gains[:, i].reshape(-1, LANES) for i in range(2)])
    gain_ride = Ride(sum_all(lax.optimization_barrier(gains.reshape(-1, LANES))))
    grad_normed = run(scatter_one(part), [out_ride, gain_ride], at={out_ride: range(left - 1)})
    moves = out_ride.moves
    qkv_sum, sent = lax.optimization_barrier((qkv_sum, [b for b, _ in moves]))
    out_ride.feed([f(b) for (_, f), b in zip(moves, sent)])
    layer_out = (hidden_own + out_ride.result).astype(bf16)
    scale_one = norm_scale(x_own_f)
    input_grad = (
        grad_hidden + norm_back(grad_normed, x_own_f * scale_one, scale_one, gain_one)
    ).astype(bf16)

    gate_grad, up_grad, down_grad = unpack(ffn_sum, 3)
    attn_sums = home(jnp.concatenate([out_sum, qkv_sum], axis=1))
    out_grad, query_grad, key_grad, value_grad = unpack([attn_sums], 4)
    while gain_ride.moves is not None:
        gain_ride.feed(exchange(gain_ride.moves))
    place = lax.axis_index(batch) * ns + lax.axis_index("seq")
    gains = lax.dynamic_slice_in_dim(gain_ride.result.reshape(2, width), place * rows, rows, 1)
    out_grad, down_grad = out_grad.T, down_grad.T
    return (
        layer_out[None],
        input_grad[None],
        attn_mass[None],
        gains[0] / low_gains[0].astype(f32),
        query_grad,
        key_grad,
        value_grad,
        out_grad,
        gains[1] / low_gains[1].astype(f32),
        gate_grad,
        up_grad,
        down_grad,
    )


def solution(mesh):
    nb, ns = mesh.shape["batch"], mesh.shape["seq"]
    mesh = jax.sharding.Mesh(mesh.devices.reshape(nb // 2, 2, ns), ("pair", "side", "seq"))
    batch = ("pair", "side")
    both = ("pair", "side", "seq")
    token_spec = P(batch, "seq", None)
    row_spec = P(both, None)
    col_spec = P(None, both)
    return jax.shard_map(
        body,
        mesh=mesh,
        in_specs=(
            token_spec,
            P(batch, "seq"),
            P(both),
            row_spec,
            row_spec,
            row_spec,
            col_spec,
            P(both),
            row_spec,
            row_spec,
            col_spec,
            token_spec,
        ),
        out_specs=(
            token_spec,
            token_spec,
            P(batch, "seq"),
            P(both),
            row_spec,
            row_spec,
            row_spec,
            col_spec,
            P(both),
            row_spec,
            row_spec,
            col_spec,
        ),
        check_vma=False,
    )
```

```python
import functools
import math

import jax
import jax.numpy as jnp
from jax import lax
from jax.experimental import pallas as pl
from jax.experimental.pallas import tpu as pltpu
from jax.sharding import PartitionSpec as P

HD = 128
LANES = 128
epsilon = 1e-05
rope_base = 10000.0
score_bias = -math.log(4096.0)
score_scale = 1.0 / math.sqrt(HD)
f32 = jnp.float32
bf16 = jnp.bfloat16
CHUNKS = 2
TILE = 256
MIB = 1 << 20


def dot(left, right):
    return jnp.dot(left, right, preferred_element_type=f32)


def dot_t(left, right):
    return lax.dot_general(left, right, (((1,), (1,)), ((), ())), preferred_element_type=f32)


def t_dot(left, right):
    return lax.dot_general(left, right, (((0,), (0,)), ((), ())), preferred_element_type=f32)


def norm_scale(values):
    return lax.rsqrt(jnp.mean(values * values, axis=-1, keepdims=True) + epsilon)


def norm_back(grad_normed, unit_rows, scale_rows, gain_vec):
    grad_unit = grad_normed * gain_vec
    return scale_rows * (
        grad_unit - unit_rows * jnp.mean(grad_unit * unit_rows, axis=-1, keepdims=True)
    )


def columns(array, at, cols):
    return pl.BlockSpec((array.shape[0], cols), lambda *_: (0, at), pipeline_mode=pl.Buffered(1))


def whole(shape):
    zeros = (0,) * len(shape)
    return pl.BlockSpec(shape, lambda *_: zeros, pipeline_mode=pl.Buffered(1))


def rows_of(tile, cols):
    return pl.BlockSpec((tile, cols), lambda i, *_: (i, 0))


def call(kernel, steps, ins, in_specs, outs, out_specs, flops, vmem=60, scalars=0):
    size = sum(math.prod(a.shape) * a.dtype.itemsize for a in (*ins, *outs))
    result = pl.pallas_call(
        kernel,
        grid_spec=pltpu.PrefetchScalarGridSpec(
            num_scalar_prefetch=scalars,
            grid=(steps,),
            in_specs=in_specs,
            out_specs=out_specs,
        ),
        out_shape=outs,
        compiler_params=pltpu.CompilerParams(
            dimension_semantics=("arbitrary",), vmem_limit_bytes=vmem * MIB
        ),
        cost_estimate=pl.CostEstimate(flops=flops, bytes_accessed=size, transcendentals=0),
    )(*ins)
    return result[0] if len(outs) == 1 else result


def pack_kernel(plans, *refs):
    ins, outs = refs[: -len(plans)], refs[-len(plans) :]
    for plan, out_ref in zip(plans, outs):
        at = 0
        for m, part, parts in plan:
            cols = ins[m].shape[1] // parts
            value = ins[m][:, part * cols : (part + 1) * cols]
            out_ref[0, :, at : at + cols] = value.astype(bf16)
            at += cols


def pack(arrays, plans, ns, marks=None):
    rows = arrays[0].shape[0]
    specs = [pl.BlockSpec((rows, a.shape[1] // ns), lambda i: (0, i)) for a in arrays]
    widths = [a.shape[1] // ns for a in arrays]
    if marks is not None:
        plans = [plan + [(len(arrays), 0, 1)] for plan in plans]
        arrays = arrays + (marks,)
        specs.append(whole(marks.shape))
        widths.append(marks.shape[1])
    cols = [sum(widths[m] // parts for m, _, parts in plan) for plan in plans]
    return call(
        functools.partial(pack_kernel, plans),
        ns,
        arrays,
        specs,
        [jax.ShapeDtypeStruct((ns, rows, n), bf16) for n in cols],
        [pl.BlockSpec((1, rows, n), lambda i: (i, 0, 0)) for n in cols],
        0,
    )


def turn(values, cosine, sine):
    return values * cosine + pltpu.roll(values, HD // 2, 1) * sine


def halves(length, cols):
    tile = min(TILE, length // 2)
    count = length // 2 // tile
    shape = jax.ShapeDtypeStruct((length // 2, cols), bf16)
    return tile, 2 * count, [shape] * 2, pair_specs(length, cols, tile)


def pair_specs(length, cols, tile):
    count = length // 2 // tile
    return [
        pl.BlockSpec((tile, cols), lambda i, *_: (jnp.minimum(i, count - 1), 0)),
        pl.BlockSpec((tile, cols), lambda i, *_: (jnp.maximum(i - count, 0), 0)),
    ]


def either(pair):
    first = pl.program_id(0) < pl.num_programs(0) // 2
    return jnp.where(first, pair[0][...], pair[1][...])


def store_half(value, outs):
    first = pl.program_id(0) < pl.num_programs(0) // 2

    @pl.when(first)
    def _():
        outs[0][...] = value

    @pl.when(jnp.logical_not(first))
    def _():
        outs[1][...] = value


def later(i, first, count):
    return jnp.clip(i - first, 0, count - 1)


def front_kernel(
    heads_all, steps, xa, xb, gain_ref, wq, wk, wv, wo, cos, sin, col, row, *refs
):
    n_ref, qo, ko, vo, oo, keep, away, qkv, mass = refs
    i = pl.program_id(0)
    tile = n_ref.shape[0]
    cols = wq.shape[1]

    @pl.when(i < steps)
    def _():
        rows = jnp.where(i < steps // 2, xa[...], xb[...]).astype(f32)
        normed = (rows * norm_scale(rows) * gain_ref[...]).astype(bf16)
        n_ref[...] = normed
        at = pl.ds(pl.multiple_of(i * tile, tile), tile)
        for j, w in enumerate((wq, wk, wv)):
            qkv[at, j * cols : (j + 1) * cols] = dot(normed, w[...])

    @pl.when(i == steps - 1)
    def _():
        cosine, sine = cos[...], sin[...]
        for h in range(cols // HD):
            head = slice(h * HD, (h + 1) * HD)
            queries = turn(qkv[:, h * HD : (h + 1) * HD], cosine, sine).astype(bf16)
            keys = turn(qkv[:, cols + h * HD : cols + (h + 1) * HD], cosine, sine).astype(bf16)
            values = qkv[:, 2 * cols + h * HD : 2 * cols + (h + 1) * HD].astype(bf16)
            qo[:, head] = queries
            ko[:, head] = keys
            vo[:, head] = values
            for j in range(steps):
                at = slice(j * tile, (j + 1) * tile)
                scores = dot_t(queries[at], keys) * score_scale + score_bias
                weights = jnp.where(row[...] <= col[at, :], jax.nn.sigmoid(scores), 0.0)
                oo[at, head] = dot(weights.astype(bf16), values).astype(bf16)
                part = jnp.sum(weights, axis=1, keepdims=True) * (1.0 / heads_all)
                part = jnp.broadcast_to(part, (tile, LANES))
                mass[at, :] = part if h == 0 else mass[at, :] + part

    def projected():
        at = pl.ds(pl.multiple_of((i - steps) * tile, tile), tile)
        value = dot_t(oo[at, :], wo[...]).astype(bf16)
        return jnp.concatenate([value, mass[at, :].astype(bf16)], axis=1)

    @pl.when((i >= steps) & (i < steps + steps // 2))
    def _():
        keep[...] = projected()

    @pl.when(i >= steps + steps // 2)
    def _():
        away[...] = projected()


def front(x_pair, gain, w_qko, w_v, cosine, sine, pos_col, pos_row, heads_all):
    length, width = 2 * x_pair[0].shape[0], x_pair[0].shape[1]
    cols = w_v.shape[1]
    tile = min(TILE, length // 2)
    steps = length // tile
    half = steps // 2
    constants = (cosine, sine, pos_col, pos_row)
    rows = jax.ShapeDtypeStruct((length, cols), bf16)
    sides = jax.ShapeDtypeStruct((length // 2, width + LANES), bf16)
    return pl.pallas_call(
        functools.partial(front_kernel, heads_all, steps),
        grid=(2 * steps,),
        in_specs=[
            pl.BlockSpec((tile, width), lambda i: (later(i, 0, half), 0)),
            pl.BlockSpec((tile, width), lambda i: (later(i, half, half), 0)),
            whole(gain.shape),
            columns(w_qko, 0, cols),
            columns(w_qko, 1, cols),
            whole(w_v.shape),
            columns(w_qko, 2, cols),
        ]
        + [whole(a.shape) for a in constants],
        out_specs=[pl.BlockSpec((tile, width), lambda i: (later(i, 0, steps), 0))]
        + [pl.BlockSpec((length, cols), lambda i: (0, 0))] * 4
        + [
            pl.BlockSpec((tile, width + LANES), lambda i: (later(i, steps, half), 0)),
            pl.BlockSpec((tile, width + LANES), lambda i: (later(i, steps + half, half), 0)),
        ],
        out_shape=[jax.ShapeDtypeStruct((length, width), bf16)] + [rows] * 4 + [sides] * 2,
        scratch_shapes=[pltpu.VMEM((length, 3 * cols), f32), pltpu.VMEM((length, LANES), f32)],
        compiler_params=pltpu.CompilerParams(
            dimension_semantics=("arbitrary",), vmem_limit_bytes=60 * MIB
        ),
        cost_estimate=pl.CostEstimate(
            flops=8 * length * width * cols,
            bytes_accessed=12 * length * width,
            transcendentals=0,
        ),
    )(*x_pair, gain, w_qko, w_qko, w_v, w_qko, *constants)


def ffn_kernel(na_ref, nb_ref, da_ref, db_ref, gu_ref, down_ref, act_ref, back_ref):
    cols = act_ref.shape[1]
    gated = dot(either((na_ref, nb_ref)), gu_ref[...])
    grad_act = dot(either((da_ref, db_ref)), down_ref[...])
    gate, up = gated[:, :cols], gated[:, cols:]
    sig = jax.nn.sigmoid(gate)
    silu = gate * sig
    act_ref[...] = (silu * up).astype(bf16)
    back_ref[:, :cols] = (grad_act * up * sig * (1.0 + gate * (1.0 - sig))).astype(bf16)
    back_ref[:, cols:] = (grad_act * silu).astype(bf16)


def ffn(n_pair, d_pair, w):
    length, width = 2 * n_pair[0].shape[0], n_pair[0].shape[1]
    cols = w.cols
    tile = min(2 * TILE, length // 2)
    return call(
        ffn_kernel,
        length // tile,
        (*n_pair, *d_pair, w.gated, w.down),
        pair_specs(length, width, tile) * 2 + w.specs(),
        [
            jax.ShapeDtypeStruct((length, cols), bf16),
            jax.ShapeDtypeStruct((length, 2 * cols), bf16),
        ],
        [rows_of(tile, cols), rows_of(tile, 2 * cols)],
        6 * length * width * cols,
    )


def cols_of(length, tile):
    return pl.BlockSpec((length, tile), lambda i, *_: (0, i))


def t_dot_pair(pair, right):
    half = pair[0].shape[0]
    return t_dot(pair[0][...], right[:half, :]) + t_dot(pair[1][...], right[half:, :])


def ffn_sums_kernel(na_ref, nb_ref, da_ref, db_ref, act_ref, back_ref, gu_ref, sum_ref, gain_ref):
    cols = act_ref.shape[1]
    gated = t_dot_pair((na_ref, nb_ref), back_ref)
    sum_ref[:, : 2 * cols] = gated.astype(bf16)
    sum_ref[:, 2 * cols :] = t_dot_pair((da_ref, db_ref), act_ref).astype(bf16)
    gain = jnp.sum(gated * gu_ref[...].astype(f32), axis=1, keepdims=True)
    gain_ref[...] = jnp.broadcast_to(gain, gain_ref.shape)


def ffn_sums(n_pair, d_pair, act, back, w):
    half, width = n_pair[0].shape
    cols = act.shape[1]
    tile = min(2 * TILE, width)
    return call(
        ffn_sums_kernel,
        width // tile,
        (*n_pair, *d_pair, act, back, w.gated),
        [cols_of(half, tile)] * 4
        + [whole(act.shape), whole(back.shape), rows_of(tile, 2 * cols)],
        [
            jax.ShapeDtypeStruct((width, 3 * cols), bf16),
            jax.ShapeDtypeStruct((width, LANES), f32),
        ],
        [rows_of(tile, 3 * cols), rows_of(tile, LANES)],
        12 * half * width * cols,
    )


def branch_sums_kernel(a_ref, b_ref, o_ref, sum_ref):
    sum_ref[...] = t_dot_pair((a_ref, b_ref), o_ref).astype(bf16)


def branch_sums(pair, attended):
    half, width = pair[0].shape
    cols = attended.shape[1]
    tile = min(2 * TILE, width)
    return call(
        branch_sums_kernel,
        width // tile,
        (*pair, attended),
        [cols_of(half, tile)] * 2 + [whole(attended.shape)],
        [jax.ShapeDtypeStruct((width, cols), bf16)],
        [rows_of(tile, cols)],
        4 * half * width * cols,
    )


def back_kernel(count, *refs):
    lefts, rights, outs = refs[:count], refs[count : 2 * count], refs[2 * count :]
    total = sum(dot_t(left[...], right[...]) for left, right in zip(lefts, rights))
    store_half(total.astype(bf16), outs)


def enter_back_kernel(*refs):
    lefts, rights, out = refs[:3], refs[3:6], refs[6]
    total = sum(dot_t(left[...], right[...]) for left, right in zip(lefts, rights))
    out[...] = total.astype(bf16)


def enter_back(lefts, w_qko, w_v, side):
    length, cols = lefts[0].shape
    width = w_v.shape[0]
    tile = min(TILE, length // 2)
    steps = length // 2 // tile
    return call(
        enter_back_kernel,
        steps,
        (*lefts, w_qko, w_qko, w_v),
        [pl.BlockSpec((tile, cols), lambda i: (i + side * steps, 0))] * 3
        + [columns(w_qko, 0, cols), columns(w_qko, 1, cols), whole(w_v.shape)],
        [jax.ShapeDtypeStruct((length // 2, width), bf16)],
        [rows_of(tile, width)],
        3 * length * width * cols,
    )


class Chunk:
    def __init__(self, gated, down, at):
        self.gated, self.down, self.at = gated, down, at
        self.cols = down.shape[1] // (at + 1)

    def specs(self):
        return [columns(self.gated, 0, 2 * self.cols), columns(self.down, self.at, self.cols)]


def back(lefts, chunks, which):
    length = lefts[0].shape[0]
    width = chunks[0].gated.shape[0]
    tile, steps, outs, specs = halves(length, width)
    return call(
        functools.partial(back_kernel, len(lefts)),
        steps,
        (*lefts, *((w.gated, w.down)[which] for w in chunks)),
        [rows_of(tile, a.shape[1]) for a in lefts] + [w.specs()[which] for w in chunks],
        outs,
        specs,
        2 * length * width * sum(a.shape[1] for a in lefts),
    )


def rear_kernel(
    steps, ba, bb, wo, q_ref, k_ref, v_ref, cos, sin, col, row, n_ref, wq, wk, wv, g0, g1, *refs
):
    dq, dk, dv, out_ref, gain_ref, grads = refs
    i = pl.program_id(0)
    tile = ba.shape[0]
    cols = wo.shape[1]

    @pl.when(i < steps)
    def _():
        at = pl.ds(pl.multiple_of(i * tile, tile), tile)
        rows = jnp.where(i < steps // 2, ba[...], bb[...])
        grads[at, :] = dot(rows, wo[...]).astype(bf16)

    @pl.when(i == steps - 1)
    def _():
        cosine, sine = cos[...], -sin[...]
        for h in range(cols // HD):
            head = slice(h * HD, (h + 1) * HD)
            queries, keys, values = q_ref[:, head], k_ref[:, head], v_ref[:, head]
            gradient = grads[:, head]
            grad_keys = grad_values = 0.0
            for j in range(steps):
                at = slice(j * tile, (j + 1) * tile)
                scores = dot_t(keys, queries[at]) * score_scale + score_bias
                weights = jnp.where(col[...] <= row[:, at], jax.nn.sigmoid(scores), 0.0)
                grad_weights = dot_t(values, gradient[at])
                grad_scores = (grad_weights * weights * (1.0 - weights)).astype(bf16)
                grad_values = grad_values + dot(weights.astype(bf16), gradient[at])
                grad_keys = grad_keys + dot(grad_scores, queries[at])
                grad_query = t_dot(grad_scores, keys) * score_scale
                dq[at, head] = turn(grad_query, cosine[at], sine[at]).astype(bf16)
            dk[:, head] = turn(grad_keys * score_scale, cosine, sine).astype(bf16)
            dv[:, head] = grad_values.astype(bf16)

    @pl.when(i >= steps)
    def _():
        gain = 0.0
        for j, (ref, w) in enumerate(((dq, wq), (dk, wk), (dv, wv))):
            part = t_dot(n_ref[...], ref[...])
            out_ref[:, j * cols : (j + 1) * cols] = part.astype(bf16)
            gain = gain + jnp.sum(part * w[...].astype(f32), axis=1, keepdims=True)
        lane = lax.broadcasted_iota(jnp.int32, g0.shape, 1)
        gain_ref[...] = jnp.where(lane == 0, gain, g0[...] + g1[...])


def rear(pair, queries, keys, values, constants, normed, w_qko, w_v, gain_sums):
    length, width = normed.shape
    cols = w_v.shape[1]
    tile = min(TILE, length // 2)
    steps = length // tile
    half = steps // 2
    block = min(2 * TILE, width)
    blocks = width // block
    rows = jax.ShapeDtypeStruct((length, cols), bf16)
    place = lambda at: pl.BlockSpec((block, cols), lambda i: (later(i, steps, blocks), at))
    return pl.pallas_call(
        functools.partial(rear_kernel, steps),
        grid=(steps + blocks,),
        in_specs=[
            pl.BlockSpec((tile, width), lambda i: (later(i, 0, half), 0)),
            pl.BlockSpec((tile, width), lambda i: (later(i, half, half), 0)),
            columns(w_qko, 2, cols),
        ]
        + [whole(a.shape) for a in (queries, keys, values, *constants)]
        + [pl.BlockSpec((length, block), lambda i: (0, later(i, steps, blocks)))]
        + [place(0), place(1), place(0)]
        + [pl.BlockSpec((block, LANES), lambda i: (later(i, steps, blocks), 0))] * 2,
        out_specs=[pl.BlockSpec((length, cols), lambda i: (0, 0))] * 3
        + [pl.BlockSpec((block, n), lambda i: (later(i, steps, blocks), 0)) for n in (3 * cols, LANES)],
        out_shape=[rows] * 3
        + [
            jax.ShapeDtypeStruct((width, 3 * cols), bf16),
            jax.ShapeDtypeStruct((width, LANES), f32),
        ],
        scratch_shapes=[pltpu.VMEM((length, cols), bf16)],
        compiler_params=pltpu.CompilerParams(
            dimension_semantics=("arbitrary",), vmem_limit_bytes=60 * MIB
        ),
        cost_estimate=pl.CostEstimate(
            flops=8 * length * width * cols,
            bytes_accessed=8 * length * width,
            transcendentals=0,
        ),
    )(*pair, w_qko, queries, keys, values, *constants, normed, w_qko, w_qko, w_v, *gain_sums)


def unpack_kernel(count, parts, *refs):
    ins, outs = refs[:count], refs[count:]
    cols = outs[0].shape[1] // count
    each = ins[0].shape[0]
    cols = cols // each
    for c, ref in enumerate(ins):
        for s in range(each):
            for i in range(parts):
                value = ref[s, :, i * cols : (i + 1) * cols].astype(f32)
                to = (s * count + c) * cols
                outs[i][:, to : to + cols] = value


def unpack(blocks, parts):
    ns, rows, cols = blocks[0].shape
    cols = cols // parts
    each = 4 if ns % 4 == 0 else 1
    return call(
        functools.partial(unpack_kernel, len(blocks), parts),
        ns // each,
        tuple(blocks),
        [pl.BlockSpec((each,) + a.shape[1:], lambda i: (i, 0, 0)) for a in blocks],
        [jax.ShapeDtypeStruct((rows, ns * len(blocks) * cols), f32)] * parts,
        [pl.BlockSpec((rows, each * len(blocks) * cols), lambda i: (0, i))] * parts,
        0,
    )


def swap_bit(block, bit, size):
    return lax.ppermute(block, "seq", [(i, i ^ bit) for i in range(size)])


def link_bits(size):
    bits = []
    bit = 2
    while bit < size:
        bits.append(bit)
        bit *= 2
    return bits


def orders(size):
    bits = link_bits(size)
    found = []
    for run in (bits, bits[::-1]):
        order = [0]
        for bit in run:
            order += [k ^ bit for k in order]
        found.append(order)
    return found


def swap_side(block):
    return lax.ppermute(block, "side", [(0, 1), (1, 0)])


def exchange(moves, waits=()):
    blocks = lax.optimization_barrier([b for b, _ in moves])
    got = [f(b) for (_, f), b in zip(moves, blocks)]
    got, values = lax.optimization_barrier((got, [box[i] for box, i in waits]))
    for (box, i), value in zip(waits, values):
        box[i] = value
    return got


def along(bit):
    return functools.partial(swap_bit, bit=bit, size=lax.axis_size("seq"))


def gather_steps(held):
    bits = link_bits(lax.axis_size("seq"))
    for pair in zip(bits, bits[::-1]):
        got = yield [(block, along(bit)) for block, bit in zip(held, pair)]
        held = [jnp.concatenate(pieces, axis=0) for pieces in zip(held, got)]
    side = jnp.concatenate(held, axis=0)
    (got,) = yield [(side, along(1))]
    return side, got


def scatter_steps(keep, away):
    bits = link_bits(lax.axis_size("seq"))
    (got,) = yield [(away, along(1))]
    length = keep.shape[0] // 2
    terms = [[t[i * length : (i + 1) * length] for t in (keep, got)] for i in range(2)]

    def total(parts, start, stop):
        return sum(t[start:stop].astype(f32) for t in parts)

    for pair in zip(bits[::-1], bits):
        sent = [total(parts, length // 2, length).astype(bf16) for parts in terms]
        got = yield [(block, along(bit)) for block, bit in zip(sent, pair)]
        length //= 2
        for parts, block in zip(terms, got):
            parts.append(block)
    return [total(parts, 0, length) for parts in terms]


def gather_one(own):
    half = own.shape[0] // 2
    return (yield from gather_steps([own[:half], own[half:]]))


def scatter_one(pair):
    blocks = yield from scatter_steps(*pair)
    return jnp.concatenate(blocks, axis=0)


def gather_two(own):
    (got,) = yield [(own, swap_side)]
    return (yield from gather_steps([own, got]))


def scatter_two(pair):
    mine, other = yield from scatter_steps(*pair)
    (got,) = yield [(other.astype(bf16), swap_side)]
    return mine + got.astype(f32)


def sum_all(block):
    bit = 1
    while bit < lax.axis_size("seq"):
        (got,) = yield [(block, along(bit))]
        block = block + got
        bit *= 2
    (got,) = yield [(block, swap_side)]
    block = block + got
    bit = 1
    while bit < lax.axis_size("pair"):
        (got,) = yield [(block, swap_pair(bit))]
        block = block + got
        bit *= 2
    return block


def swap_pair(bit):
    pairs = [(i, i ^ bit) for i in range(lax.axis_size("pair"))]
    return lambda block: lax.ppermute(block, "pair", pairs)


class Ride:
    def __init__(self, steps):
        self.steps = steps
        self.result = None
        self.feed(None)

    def feed(self, got):
        try:
            self.moves = self.steps.send(got)
        except StopIteration as end:
            self.moves, self.result = None, end.value


def run(steps, riders=(), waits=(), then=(), at=None):
    main = steps if isinstance(steps, Ride) else Ride(steps)
    waits, then = list(waits), list(then)
    stage = 0
    while main.moves is not None:
        riding = [r for r in riders if at is None or stage in at.get(r, range(8))]
        active = [main] + [rider for rider in riding if rider.moves is not None]
        stage += 1
        got = exchange(
            [move for ride in active for move in ride.moves], waits.pop(0) if waits else ()
        )
        for ride in active:
            part, got = got[: len(ride.moves)], got[len(ride.moves) :]
            ride.feed(part)
        if then:
            then.pop(0)()
    return main.result


def body(
    tokens,
    positions,
    gain_attn,
    query_weight,
    key_weight,
    value_weight,
    out_weight,
    gain_ffn,
    gate_weight,
    up_weight,
    down_weight,
    cotangent,
):
    ns = lax.axis_size("seq")
    nb = lax.axis_size("pair") * lax.axis_size("side")
    batch = ("pair", "side")
    near = ("side", "seq")
    rows, width = query_weight.shape
    hidden = gate_weight.shape[1]
    head_cols = width // ns
    heads = head_cols // HD
    ffn_cols = hidden // (2 * ns * CHUNKS)
    own = tokens.shape[1]

    def swap(blocks, axes="seq"):
        return lax.all_to_all(blocks, axes, split_axis=0, concat_axis=0, tiled=True)

    def gather_z(block, axes=batch):
        return lax.all_gather(block, axes, axis=0, tiled=True)

    def scatter_z(full, axes=batch):
        return lax.psum_scatter(full, axes, scatter_dimension=0, tiled=True)

    low_gains = [gain_attn.astype(bf16), gain_ffn.astype(bf16)]
    gain_cols = jnp.pad(jnp.stack(low_gains, axis=1), ((0, 0), (0, LANES - 2)))
    w_v = gather_z(jnp.concatenate([value_weight.astype(bf16), gain_cols], axis=1))

    place = positions[0]
    marks = jnp.stack([place // 128, place % 128]).astype(bf16)
    marks = jnp.pad(marks.reshape(2, -1, LANES)[:, 0], ((0, rows - 2), (0, 0)))
    attn_blocks = pack(
        (query_weight, key_weight, out_weight.T.astype(bf16)),
        [[(m, 0, 1) for m in range(3)]],
        ns,
        marks,
    )
    attn_blocks = swap(attn_blocks)
    plans = [[(m, c, CHUNKS) for m in range(3)] for c in range(CHUNKS)]
    ffn_blocks = list(pack((gate_weight, up_weight, down_weight.T.astype(bf16)), plans, 2 * ns))
    x_own, attn_blocks = lax.optimization_barrier((tokens[0], attn_blocks))
    x_ride, dy_ride = Ride(gather_one(x_own)), Ride(gather_two(cotangent[0]))
    got = exchange(x_ride.moves + dy_ride.moves)
    x_ride.feed(got[:-1])
    dy_ride.feed(got[-1:])
    x_all = run(x_ride)
    w_v = w_v.reshape(nb, rows, -1)
    spread = jnp.broadcast_to(w_v[None, :, :, width:], (ns, nb, rows, LANES))
    w_v = w_v[:, :, :width].reshape(nb, rows, ns, head_cols).transpose(2, 0, 1, 3)
    w_v = swap(jnp.concatenate([w_v, spread], axis=3))
    w_v = w_v.transpose(1, 0, 2, 3).reshape(width, -1)
    gain_one = w_v[:, head_cols].astype(f32)
    gain_two = w_v[:, head_cols + 1].astype(f32)
    w_v = w_v[:, :head_cols]

    around = jnp.array([[[k ^ core for k in order] for order in orders(ns)] for core in range(2)])
    around = lax.axis_index("seq") ^ around.astype(jnp.int32)
    place = attn_blocks[:, :2, -LANES:].astype(f32).astype(jnp.int32)
    place = (place[:, 0] * 128 + place[:, 1]).reshape(ns, 2, own // 2)
    place = jnp.stack([jnp.take(place[:, i], around[:, i], axis=0) for i in range(2)], axis=1)
    place = place.reshape(-1)
    half_size = HD // 2
    frequency = jnp.exp(jnp.arange(half_size).astype(f32) * (-2.0 * math.log(rope_base) / HD))
    angles = place.astype(f32)[:, None] * frequency[None, :]
    cosine, sine = jnp.cos(angles), jnp.sin(angles)
    cosine = jnp.concatenate([cosine, cosine], axis=1)
    sine = jnp.concatenate([-sine, sine], axis=1)
    pos_col, pos_row = place[:, None], place[None, :]

    attn_blocks = attn_blocks.reshape(ns * rows, -1)
    w_qko = gather_z(attn_blocks[:, : 3 * head_cols])
    (w_qko, w_v, gain_one, x_all, cosine, sine, pos_col, pos_row, ffn_blocks[0]) = (
        lax.optimization_barrier(
            (w_qko, w_v, gain_one, x_all, cosine, sine, pos_col, pos_row, ffn_blocks[0])
        )
    )
    ffn_blocks[0] = swap(ffn_blocks[0], near).reshape(2 * ns * rows, -1)

    constants = (cosine, sine, pos_col, pos_row)
    normed, queries, keys, values, attended, kept, away = front(
        x_all, gain_one[None], w_qko, w_v, *constants, width // HD
    )
    w_ffn = [gather_z(ffn_blocks[0], "pair")]

    def second():
        ffn_blocks[1] = swap(ffn_blocks[1], near).reshape(2 * ns * rows, -1)

    attn_own = run(
        scatter_one((kept, away)),
        [dy_ride],
        [[(ffn_blocks, 1)], [(w_ffn, 0), (ffn_blocks, 1)]],
        [second],
    )
    w_ffn.append(gather_z(ffn_blocks[1][:, : 2 * ffn_cols], "pair"))
    w_ffn.append(gather_z(ffn_blocks[1][:, 2 * ffn_cols :], "pair"))
    attn_mass = attn_own[:, width]
    x_own_f = x_own.astype(f32)
    hidden_own = x_own_f + attn_own[:, :width]
    scale_two = norm_scale(hidden_own)
    unit_two = hidden_own * scale_two
    normed_ffn = run(
        gather_two((unit_two * gain_two).astype(bf16)),
        [dy_ride],
        [[], [(w_ffn, 1)]],
    )
    dy_all = dy_ride.result

    acts, backs, sums, gain_sums = [], [], [], []
    chunks = [Chunk(w_ffn[0], w_ffn[0], 2)]
    for c in range(CHUNKS):
        act, grads = ffn(normed_ffn, dy_all, chunks[c])
        acts.append(act)
        backs.append(grads)
        if c + 1 == CHUNKS:
            break
        part, gains = ffn_sums(normed_ffn, dy_all, act, grads, chunks[c])
        gain_sums.append(gains)
        acts[c], backs[c], part, w_ffn[1:] = lax.optimization_barrier(
            (act, grads, part, w_ffn[1:])
        )
        chunks.append(Chunk(w_ffn[1], w_ffn[2], 0))
        sums.append(scatter_z(part, "pair"))
    grads_pair = back(backs, chunks, 0)

    def home(part, axes="seq"):
        return swap(part.reshape(lax.axis_size(axes), rows, -1), axes)

    made = []

    def last_sums():
        part, gains = ffn_sums(normed_ffn, dy_all, acts[-1], backs[-1], chunks[-1])
        gain_sums.append(gains)
        made.append(part)

    def leave():
        sums.append(scatter_z(made[0], "pair"))

    def output():
        made.append(back(acts, chunks, 1))

    grad_normed_two = run(
        scatter_two(grads_pair),
        (),
        [[(acts, 1), (backs, 1)], [(made, 0)], [(sums, 0), (acts, 0)], [(made, 1)]],
        [last_sums, leave, output],
    )
    grad_hidden = cotangent[0].astype(f32) + norm_back(
        grad_normed_two, unit_two, scale_two, gain_two
    )

    ffn_sum = [home(sums[0], near)]
    out_ride = Ride(scatter_two(made[1]))
    waits = [[], [(ffn_sum, 0), (sums, 1)]]
    left = len(link_bits(ns))
    branch = run(gather_one(grad_hidden.astype(bf16)), [out_ride], waits, (), {out_ride: (left,)})
    out_sum = branch_sums(branch, attended)
    moves = out_ride.moves
    branch, out_sum, sent = lax.optimization_barrier((branch, out_sum, [b for b, _ in moves]))
    flying = [f(b) for (_, f), b in zip(moves, sent)]
    out_sum = scatter_z(out_sum)
    dq, dk, dv, qkv_local, gains = rear(
        branch, queries, keys, values, constants, normed, w_qko, w_v, gain_sums
    )
    ffn_sum.append(home(sums[1], near))
    dq, dk, dv, qkv_local, ffn_sum, flying, out_sum = lax.optimization_barrier(
        (dq, dk, dv, qkv_local, ffn_sum, flying, out_sum)
    )
    out_ride.feed(flying)
    qkv_sum = scatter_z(qkv_local)
    away = enter_back([dq, dk, dv], w_qko, w_v, 1)
    part = (enter_back([dq, dk, dv], w_qko, w_v, 0), away)
    gains = jnp.stack([gains[:, i].reshape(-1, LANES) for i in range(2)])
    gain_ride = Ride(sum_all(lax.optimization_barrier(gains.reshape(-1, LANES))))
    grad_normed = run(scatter_one(part), [out_ride, gain_ride], at={out_ride: range(left - 1)})
    moves = out_ride.moves
    qkv_sum, sent = lax.optimization_barrier((qkv_sum, [b for b, _ in moves]))
    out_ride.feed([f(b) for (_, f), b in zip(moves, sent)])
    layer_out = (hidden_own + out_ride.result).astype(bf16)
    scale_one = norm_scale(x_own_f)
    input_grad = (
        grad_hidden + norm_back(grad_normed, x_own_f * scale_one, scale_one, gain_one)
    ).astype(bf16)

    gate_grad, up_grad, down_grad = unpack(ffn_sum, 3)
    attn_sums = home(jnp.concatenate([out_sum, qkv_sum], axis=1))
    out_grad, query_grad, key_grad, value_grad = unpack([attn_sums], 4)
    while gain_ride.moves is not None:
        gain_ride.feed(exchange(gain_ride.moves))
    place = lax.axis_index(batch) * ns + lax.axis_index("seq")
    gains = lax.dynamic_slice_in_dim(gain_ride.result.reshape(2, width), place * rows, rows, 1)
    out_grad, down_grad = out_grad.T, down_grad.T
    return (
        layer_out[None],
        input_grad[None],
        attn_mass[None],
        gains[0] / low_gains[0].astype(f32),
        query_grad,
        key_grad,
        value_grad,
        out_grad,
        gains[1] / low_gains[1].astype(f32),
        gate_grad,
        up_grad,
        down_grad,
    )


def solution(mesh):
    nb, ns = mesh.shape["batch"], mesh.shape["seq"]
    mesh = jax.sharding.Mesh(mesh.devices.reshape(nb // 2, 2, ns), ("pair", "side", "seq"))
    batch = ("pair", "side")
    both = ("pair", "side", "seq")
    token_spec = P(batch, "seq", None)
    row_spec = P(both, None)
    col_spec = P(None, both)
    return jax.shard_map(
        body,
        mesh=mesh,
        in_specs=(
            token_spec,
            P(batch, "seq"),
            P(both),
            row_spec,
            row_spec,
            row_spec,
            col_spec,
            P(both),
            row_spec,
            row_spec,
            col_spec,
            token_spec,
        ),
        out_specs=(
            token_spec,
            token_spec,
            P(batch, "seq"),
            P(both),
            row_spec,
            row_spec,
            row_spec,
            col_spec,
            P(both),
            row_spec,
            row_spec,
            col_spec,
        ),
        check_vma=False,
    )
```
